32 devices in a mesh: dp: 16 (over z, y, x), head: 2 (over core).
Axes of the slice: x: 2, y: 2, z: 4, core: 2. Of those that a mesh axis runs over, the one named last changes fastest.
Arguments:
- tokens: bfloat16 [50176, 384], P('dp'), may hold values from -6 to 6
- keep: int32 [256, 2], P('dp'), may hold values 0 or 1
- cotangent: bfloat16 [50176, 384], P(('dp', 'head')), may hold values from -6 to 6
- input_weight: float32 [3, 384, 384], P(None, 'dp', 'head'), may hold values from -0.3125 to 0.3125
- output_weight: float32 [384, 384], P('head', 'dp'), may hold values from -1.25 to 1.25
- expand_weight: float32 [384, 1536], P(None, ('dp', 'head')), may hold values from -0.3125 to 0.3125
- shrink_weight: float32 [1536, 384], P(('dp', 'head')), may hold values from -0.15625 to 0.15625
- bias_tables: float32 [12, 530], P('head'), may hold values from -4 to 4
- vectors: float32 [12, 384], replicated, may hold values from -0.6 to 1.6
- first_input: float32 [3, 384, 384], P(None, 'dp', 'head'), may hold values from -80 to 80
- second_input: float32 [3, 384, 384], P(None, 'dp', 'head'), may hold values from 6.272 to 100.352
- average_input: float32 [3, 384, 384], P(None, 'dp', 'head'), may hold values from -0.3125 to 0.3125
- first_output: float32 [384, 384], P('head', 'dp'), may hold values from -40 to 40
- second_output: float32 [384, 384], P('head', 'dp'), may hold values from 1.568 to 25.088
- average_output: float32 [384, 384], P('head', 'dp'), may hold values from -1.25 to 1.25
- first_expand: float32 [384, 1536], P(None, ('dp', 'head')), may hold values from -80 to 80
- second_expand: float32 [384, 1536], P(None, ('dp', 'head')), may hold values from 6.272 to 100.352
- average_expand: float32 [384, 1536], P(None, ('dp', 'head')), may hold values from -0.3125 to 0.3125
- first_shrink: float32 [1536, 384], P(('dp', 'head')), may hold values from -80 to 80
- second_shrink: float32 [1536, 384], P(('dp', 'head')), may hold values from 6.272 to 100.352
- average_shrink: float32 [1536, 384], P(('dp', 'head')), may hold values from -0.15625 to 0.15625
- first_tables: float32 [12, 530], P('head'), may hold values from -16 to 16
- second_tables: float32 [12, 530], P('head'), may hold values from 0.25088 to 4.01408
- average_tables: float32 [12, 530], P('head'), may hold values from -4 to 4
- first_vectors: float32 [12, 384], replicated, may hold values from -160 to 160
- second_vectors: float32 [12, 384], replicated, may hold values from 25.088 to 401.408
- average_vectors: float32 [12, 384], replicated, may hold values from -0.6 to 1.6
Outputs:
- result: float32 [50176, 384], P(('dp', 'head'))
- input_grad: float32 [50176, 384], P(('dp', 'head'))
- input_new: float32 [3, 384, 384], P(None, 'dp', 'head')
- input_first: float32 [3, 384, 384], P(None, 'dp', 'head')
- input_second: float32 [3, 384, 384], P(None, 'dp', 'head')
- input_average: float32 [3, 384, 384], P(None, 'dp', 'head')
- input_copy: bfloat16 [3, 384, 384], P(None, 'dp', 'head')
- output_new: float32 [384, 384], P('head', 'dp')
- output_first: float32 [384, 384], P('head', 'dp')
- output_second: float32 [384, 384], P('head', 'dp')
- output_average: float32 [384, 384], P('head', 'dp')
- output_copy: bfloat16 [384, 384], P('head', 'dp')
- expand_new: float32 [384, 1536], P(None, ('dp', 'head'))
- expand_first: float32 [384, 1536], P(None, ('dp', 'head'))
- expand_second: float32 [384, 1536], P(None, ('dp', 'head'))
- expand_average: float32 [384, 1536], P(None, ('dp', 'head'))
- expand_copy: bfloat16 [384, 1536], P(None, ('dp', 'head'))
- shrink_new: float32 [1536, 384], P(('dp', 'head'))
- shrink_first: float32 [1536, 384], P(('dp', 'head'))
- shrink_second: float32 [1536, 384], P(('dp', 'head'))
- shrink_average: float32 [1536, 384], P(('dp', 'head'))
- shrink_copy: bfloat16 [1536, 384], P(('dp', 'head'))
- tables_new: float32 [12, 530], P('head')
- tables_first: float32 [12, 530], P('head')
- tables_second: float32 [12, 530], P('head')
- tables_average: float32 [12, 530], P('head')
- vectors_new: float32 [12, 384], replicated
- vectors_first: float32 [12, 384], replicated
- vectors_second: float32 [12, 384], replicated
- vectors_average: float32 [12, 384], replicated
The draws below stay inside these ranges and needn't reach their ends.
All inputs are finite; a program needn't handle non-finite values. No bound on the sum of `keep` on one device may be relied on, other than what follows from the above.
Results may differ from the reference program's by a relative error of at most 0.014.
The reference program's roundings to bfloat16 on the way count: a program that leaves them out, or rounds other values in their place, can miss the bound.
Values may be sent and summed in bfloat16 or wider, within the bound.
No kernel may reach another device: no remote copies, remote signals or barrier semaphores. Data moves between devices by JAX's collectives and lax.ppermute only.
A program may use at most 384 MiB of HBM per device.

```python
import math
import jax
import jax.numpy as jnp
import numpy as np
from jax import lax

D = 384
HEADS = 12
HEAD_DIM = 32
FF = 1536
SIDE = 14
WINDOW = 7
FINE = 13
STEP = 10
IMAGES = 256
TOKENS = 50176
TABLE = 530
VROWS = 12


def shape_vectors(noise):
    rows = 8 + FF // D
    number = jnp.arange(rows)
    gains = (number == 0) | (number == 5)
    return jnp.where(gains[:, None], 1.0 + 0.2 * noise, 0.2 * noise)


def draw_vectors(key, part):
    key = jax.random.fold_in(key, 1)
    rows = 8 + FF // D
    noise = jnp.clip(jax.random.normal(key, (rows, D), jnp.float32), -3.0, 3.0)
    return shape_vectors(noise)


def draw_average_vectors(key, part):
    key = jax.random.fold_in(key, 2)
    rows = 8 + FF // D
    noise = jnp.clip(jax.random.normal(key, (rows, D), jnp.float32), -3.0, 3.0)
    return shape_vectors(noise)


def with_ends(drawn, stream_key, least, high):
    longest = drawn.shape.index(max(drawn.shape))
    spots = []
    for shift in (0, 1):
        where = [jax.random.randint(jax.random.fold_in(stream_key, axis), (), 0, length) for axis, length in enumerate(drawn.shape)]
        where[longest] = (where[longest] + shift) % drawn.shape[longest]
        spots.append(tuple(where))
    return drawn.at[spots[0]].set(least).at[spots[1]].set(high)


def steps_of(rng, dims, pieces, least, largest):
    level, own = 1.0, jax.random.fold_in(rng, 6)
    for position, parts in pieces:
        steps = jnp.exp(jax.random.uniform(jax.random.fold_in(own, position), (parts,), jnp.float32, least / len(pieces), largest / len(pieces)))
        level = level * jnp.repeat(steps, dims[position] // parts).reshape([-1 if axis == position else 1 for axis in range(len(dims))])
    return level


def gaussian(own_key, dims, scale, reach, split=(), kind=jnp.bfloat16):
    drawn = jax.random.normal(own_key, dims, jnp.float32) * scale
    if len(split) > 0:
        drawn = steps_of(own_key, dims, split, -0.22, 0.18) * drawn
    return jnp.clip(drawn, min=-reach, max=reach).astype(kind)


def setup_inputs(seed: int = 0) -> dict:
    splits = jax.random.split(jax.random.key(seed), 28)
    tokens = gaussian(splits[0], (TOKENS, D), 1.0, 6.0, ((0, 16),))
    keep = with_ends((jax.random.randint(splits[1], (IMAGES, 2), 0, 5) < 4).astype(jnp.int32), jax.random.fold_in(splits[1], 1), 0, 1)
    cotangent = gaussian(splits[2], (TOKENS, D), 1.0, 6.0, ((0, 32),))
    input_weight = gaussian(splits[3], (3, D, D), D ** -0.5, 0.3125, ((1, 16), (2, 2)), jnp.float32)
    output_weight = gaussian(splits[4], (D, D), (D // 16) ** -0.5, 1.25, ((0, 2), (1, 16)), jnp.float32)
    expand_weight = gaussian(splits[5], (D, FF), D ** -0.5, 0.3125, ((1, 32),), jnp.float32)
    shrink_weight = gaussian(splits[6], (FF, D), FF ** -0.5, 0.15625, ((0, 32),), jnp.float32)
    bias_tables = gaussian(splits[7], (HEADS, TABLE), 1.0, 4.0, ((0, 2),), jnp.float32)
    vectors = draw_vectors(jax.random.fold_in(splits[27], 71), 0)
    first_input = gaussian(splits[9], (3, D, D), (0.055 * TOKENS ** 0.5), 80.0, ((1, 16), (2, 2)), jnp.float32)
    second_input = jnp.clip(jnp.exp(math.log(100.352) - 2.7725887 * jax.random.uniform(splits[10], (3, D, D), jnp.float32) ** steps_of(splits[10], (3, D, D), ((1, 16), (2, 2)), -0.2, 0.2)), 6.272, 100.352)
    average_input = gaussian(splits[11], (3, D, D), D ** -0.5, 0.3125, ((1, 16), (2, 2)), jnp.float32)
    first_output = gaussian(splits[12], (D, D), (0.0275 * TOKENS ** 0.5), 40.0, ((0, 2), (1, 16)), jnp.float32)
    second_output = jnp.clip(jnp.exp(math.log(25.088) - 2.7725887 * jax.random.uniform(splits[13], (D, D), jnp.float32) ** steps_of(splits[13], (D, D), ((0, 2), (1, 16)), -0.2, 0.2)), 1.568, 25.088)
    average_output = gaussian(splits[14], (D, D), (D // 16) ** -0.5, 1.25, ((0, 2), (1, 16)), jnp.float32)
    first_expand = gaussian(splits[15], (D, FF), (0.055 * TOKENS ** 0.5), 80.0, ((1, 32),), jnp.float32)
    second_expand = jnp.clip(jnp.exp(math.log(100.352) - 2.7725887 * jax.random.uniform(splits[16], (D, FF), jnp.float32) ** steps_of(splits[16], (D, FF), ((1, 32),), -0.2, 0.2)), 6.272, 100.352)
    average_expand = gaussian(splits[17], (D, FF), D ** -0.5, 0.3125, ((1, 32),), jnp.float32)
    first_shrink = gaussian(splits[18], (FF, D), (0.055 * TOKENS ** 0.5), 80.0, ((0, 32),), jnp.float32)
    second_shrink = jnp.clip(jnp.exp(math.log(100.352) - 2.7725887 * jax.random.uniform(splits[19], (FF, D), jnp.float32) ** steps_of(splits[19], (FF, D), ((0, 32),), -0.2, 0.2)), 6.272, 100.352)
    average_shrink = gaussian(splits[20], (FF, D), FF ** -0.5, 0.15625, ((0, 32),), jnp.float32)
    first_tables = gaussian(splits[21], (HEADS, TABLE), (0.011 * TOKENS ** 0.5), 16.0, ((0, 2),), jnp.float32)
    second_tables = jnp.clip(jnp.exp(math.log(4.01408) - 2.7725887 * jax.random.uniform(splits[22], (HEADS, TABLE), jnp.float32) ** steps_of(splits[22], (HEADS, TABLE), ((0, 2),), -0.2, 0.2)), 0.25088, 4.01408)
    average_tables = gaussian(splits[23], (HEADS, TABLE), 1.0, 4.0, ((0, 2),), jnp.float32)
    first_vectors = gaussian(splits[24], (VROWS, D), (0.11 * TOKENS ** 0.5), 160.0, (), jnp.float32)
    second_vectors = jnp.clip(jnp.exp(jax.random.uniform(splits[25], (VROWS, D), jnp.float32, math.log(25.088), math.log(401.408))), 25.088, 401.408)
    average_vectors = draw_average_vectors(jax.random.fold_in(splits[27], 71), 0)
    return dict(tokens=tokens, keep=keep, cotangent=cotangent, input_weight=input_weight, output_weight=output_weight, expand_weight=expand_weight, shrink_weight=shrink_weight, bias_tables=bias_tables, vectors=vectors, first_input=first_input, second_input=second_input, average_input=average_input, first_output=first_output, second_output=second_output, average_output=average_output, first_expand=first_expand, second_expand=second_expand, average_expand=average_expand, first_shrink=first_shrink, second_shrink=second_shrink, average_shrink=average_shrink, first_tables=first_tables, second_tables=second_tables, average_tables=average_tables, first_vectors=first_vectors, second_vectors=second_vectors, average_vectors=average_vectors)


@jax.custom_vjp
def low(v):
    return lax.optimization_barrier(v.astype(jnp.bfloat16)).astype(jnp.float32)

@jax.custom_vjp
def low_back(v):
    return v

def low_keep(v):
    return (low(v), None)

def low_pass(kept, grad):
    return (grad,)

def back_keep(v):
    return (v, None)

def back_low(kept, grad):
    return (low(grad),)
low.defvjp(low_keep, low_pass)
low_back.defvjp(back_keep, back_low)
DROP_SCALE = 1.25
HIGHEST = lax.Precision.HIGHEST

def focal_tables():
    half = SIDE // 2
    across = SIDE // WINDOW
    margin = (FINE - WINDOW) // 2
    span = WINDOW + FINE - 1
    coarse_span = SIDE - 1
    cells = np.arange(WINDOW * WINDOW)
    query_row = cells // WINDOW
    query_col = cells % WINDOW
    places = np.arange(FINE * FINE)
    key_row = places // FINE
    key_col = places % FINE
    near_index = (key_row[None, :] - query_row[:, None] + WINDOW - 1) * span + (key_col[None, :] - query_col[:, None] + WINDOW - 1)
    pooled = np.arange(half * half)
    pool_row = pooled // half
    pool_col = pooled % half
    index_list = []
    mask_list = []
    for row in range(across):
        for col in range(across):
            row_abs = row * WINDOW + query_row
            col_abs = col * WINDOW + query_col
            far_index = span * span + (row_abs[:, None] // 2 - pool_row[None, :] + half - 1) * coarse_span + (col_abs[:, None] // 2 - pool_col[None, :] + half - 1)
            index_list.append(np.concatenate([near_index, far_index], axis=1))
            key_row_abs = row * WINDOW - margin + key_row
            key_col_abs = col * WINDOW - margin + key_col
            inside = (key_row_abs >= 0) & (key_row_abs < SIDE) & (key_col_abs >= 0) & (key_col_abs < SIDE)
            mask_list.append(np.concatenate([np.where(inside, 0.0, -1000000000.0), np.zeros(half * half)]))
    return (np.stack(index_list).astype(np.int32), np.stack(mask_list).astype(np.float32))

def attend(mixed, table):
    count = mixed.shape[1] // (SIDE * SIDE)
    heads = table.shape[0]
    half = SIDE // 2
    across = SIDE // WINDOW
    windows = across * across
    margin = (FINE - WINDOW) // 2
    maps = mixed.reshape(3, count, SIDE, SIDE, heads, HEAD_DIM)
    query = low(maps[0])
    pooled = low(lax.optimization_barrier(jnp.mean(maps[1:].reshape(2, count, half, 2, half, 2, heads, HEAD_DIM), axis=(3, 5))))
    fine = jnp.pad(low(maps[1:]), ((0, 0), (0, 0), (margin, margin), (margin, margin), (0, 0), (0, 0)))
    blocks = [fine[:, :, row * WINDOW:row * WINDOW + FINE, col * WINDOW:col * WINDOW + FINE] for row in range(across) for col in range(across)]
    near = jnp.stack(blocks, axis=2).reshape(2, count, windows, FINE * FINE, heads, HEAD_DIM)
    far = jnp.broadcast_to(pooled.reshape(2, count, 1, half * half, heads, HEAD_DIM), (2, count, windows, half * half, heads, HEAD_DIM))
    context = jnp.concatenate([near, far], axis=3)
    queries = query.reshape(count, across, WINDOW, across, WINDOW, heads, HEAD_DIM).transpose(0, 1, 3, 2, 4, 5, 6)
    queries = queries.reshape(count, windows, WINDOW * WINDOW, heads, HEAD_DIM)
    index, blocked = focal_tables()
    bias = jnp.transpose(table[:, index], (1, 0, 2, 3))
    scores = jnp.einsum('bwqhd,bwkhd->bwhqk', queries, context[0], precision=HIGHEST) * HEAD_DIM ** (-0.5)
    scores = low_back(scores + bias[None] + blocked[None, :, None, None, :])
    top = lax.optimization_barrier(jnp.max(scores, axis=-1, keepdims=True))
    weights = jnp.exp(scores - top)
    probs = low(weights / lax.optimization_barrier(jnp.sum(weights, axis=-1, keepdims=True)))
    attended = jnp.einsum('bwhqk,bwkhd->bwqhd', probs, context[1], precision=HIGHEST)
    attended = attended.reshape(count, across, across, WINDOW, WINDOW, heads, HEAD_DIM).transpose(0, 1, 3, 2, 4, 5, 6)
    return attended.reshape(count * SIDE * SIDE, heads * HEAD_DIM)

def layer_norm(stream, gain, shift):
    center = stream - lax.optimization_barrier(jnp.mean(stream, axis=-1, keepdims=True))
    spread = lax.optimization_barrier(jnp.mean(center * center, axis=-1, keepdims=True))
    return center * lax.rsqrt(spread + 1e-05) * gain + shift

def forward(stream, input_weight, output_weight, expand_weight, shrink_weight, tables, vectors, keep_attn, keep_mlp):
    ln_one = low(layer_norm(stream, vectors[0], vectors[1]))
    bias = jnp.stack([vectors[2], jnp.zeros_like(vectors[2]), vectors[3]])
    mixed = jnp.einsum('nd,tdc->tnc', ln_one, low(input_weight), precision=HIGHEST) + bias[:, None, :]
    mixed = low_back(mixed)
    groups = mixed.reshape(3, IMAGES // 16, 16 * SIDE * SIDE, D).transpose(1, 0, 2, 3)
    attended = lax.map(jax.checkpoint(lambda group: attend(group, tables)), groups).reshape(TOKENS, D)
    attended = low_back(low(attended))
    branch = low_back(jnp.dot(attended, low(output_weight), precision=HIGHEST))
    state = stream + keep_attn * DROP_SCALE * (branch + vectors[4])
    ln_two = low(layer_norm(state, vectors[5], vectors[6]))
    pre = low_back(jnp.dot(ln_two, low(expand_weight), precision=HIGHEST) + vectors[8:].reshape(FF))
    act = low(jax.nn.gelu(pre, approximate=False))
    out = low_back(jnp.dot(act, low(shrink_weight), precision=HIGHEST))
    return state + keep_mlp * DROP_SCALE * (out + vectors[7])

def adamw(weight, grad, first, second, average, rate, decay):
    first = 0.9 * first + 0.1 * grad
    second = 0.999 * second + 0.001 * grad * grad
    fix_one = 1.0 - 0.9 ** STEP
    fix_two = 1.0 - 0.999 ** STEP
    weight = weight - rate * (first / fix_one / (jnp.sqrt(second / fix_two) + 1e-08) + decay * weight)
    average = 0.9 * average + 0.1 * weight
    return (weight, first, second, average)

def reference(tokens, keep, cotangent, input_weight, output_weight, expand_weight, shrink_weight, bias_tables, vectors, first_input, second_input, average_input, first_output, second_output, average_output, first_expand, second_expand, average_expand, first_shrink, second_shrink, average_shrink, first_tables, second_tables, average_tables, first_vectors, second_vectors, average_vectors):
    flags = keep.astype(jnp.float32)
    keep_attn = jnp.repeat(flags[:, 0], SIDE * SIDE)[:, None]
    keep_mlp = jnp.repeat(flags[:, 1], SIDE * SIDE)[:, None]

    def run(stream, w_in, w_out, w_expand, w_shrink, tables, vecs):
        return forward(stream, w_in, w_out, w_expand, w_shrink, tables, vecs, keep_attn, keep_mlp)
    result, pull = jax.vjp(run, tokens.astype(jnp.float32), input_weight, output_weight, expand_weight, shrink_weight, bias_tables, vectors)
    grads = pull(cotangent.astype(jnp.float32))
    input_new = adamw(input_weight, grads[1], first_input, second_input, average_input, 0.06, 0.05)
    output_new = adamw(output_weight, grads[2], first_output, second_output, average_output, 0.3, 0.05)
    expand_new = adamw(expand_weight, grads[3], first_expand, second_expand, average_expand, 0.06, 0.05)
    shrink_new = adamw(shrink_weight, grads[4], first_shrink, second_shrink, average_shrink, 0.06, 0.05)
    tables_new = adamw(bias_tables, grads[5], first_tables, second_tables, average_tables, 1.0, 0.0)
    vectors_new = adamw(vectors, grads[6], first_vectors, second_vectors, average_vectors, 0.6, 0.0)
    return (result, grads[0], input_new[0], input_new[1], input_new[2], input_new[3], input_new[0].astype(jnp.bfloat16), output_new[0], output_new[1], output_new[2], output_new[3], output_new[0].astype(jnp.bfloat16), expand_new[0], expand_new[1], expand_new[2], expand_new[3], expand_new[0].astype(jnp.bfloat16), shrink_new[0], shrink_new[1], shrink_new[2], shrink_new[3], shrink_new[0].astype(jnp.bfloat16), tables_new[0], tables_new[1], tables_new[2], tables_new[3], vectors_new[0], vectors_new[1], vectors_new[2], vectors_new[3])
```

```python
from functools import partial

import jax
import jax.numpy as jnp
import numpy as np
from jax import lax
from jax.experimental import pallas as pl
from jax.experimental.pallas import tpu as pltpu
from jax.sharding import PartitionSpec as P

HEAD_DIM = 32
SIDE = 14
WINDOW = 7
FINE = 13
STEP = 10
DROP_SCALE = 1.25

CELLS = SIDE * SIDE
HALF = SIDE // 2
POOL = HALF * HALF
SPAN = WINDOW + FINE - 1
FAR_SPAN = SIDE - 1
ROWS = 208
WIDE = 256
TOP = WINDOW * SIDE
OFFSET = CELLS - (WINDOW + (FINE - WINDOW) // 2) * SIDE
NEAR = CELLS - OFFSET
SLOTS = 192
LANES = 128
GROUP = LANES // HEAD_DIM
PAIR = 2
MANY = 4
SCALE = HEAD_DIM**-0.5
TO_LOG2 = SCALE * 1.4426950408889634
LINE = 384
CENTRE = 192
FAR_CENTRE = 64
FAR_ROW = NEAR // 8 * 8

BF = jnp.bfloat16
F32 = jnp.float32


def nn(a, b, **kw):
    return lax.dot_general(a, b, (((1,), (0,)), ((), ())), preferred_element_type=F32, **kw)


def nt(a, b, **kw):
    return lax.dot_general(a, b, (((1,), (1,)), ((), ())), preferred_element_type=F32, **kw)


def split(v):
    high = v.astype(BF)
    return high, (v - high.astype(F32)).astype(BF)


def cost(micros, bytes_accessed=0):
    return pl.CostEstimate(
        flops=int(micros * 1.15e9), bytes_accessed=bytes_accessed, transcendentals=0
    )


def params(mebibytes):
    return pltpu.CompilerParams(vmem_limit_bytes=mebibytes * 2**20)


def kinds():
    q = np.arange(CELLS)
    qr, qc = q // SIDE, q % SIDE
    margin = (FINE - WINDOW) // 2
    low_r, low_c = qr // WINDOW * WINDOW - margin, qc // WINDOW * WINDOW - margin
    key = np.arange(NEAR)[:, None] + np.where(q < TOP, 0, OFFSET)[None]
    kr, kc = key // SIDE, key % SIDE
    inside = (kr >= low_r) & (kr < low_r + FINE) & (kc >= low_c) & (kc < low_c + FINE)
    kind = np.zeros((SLOTS, WIDE), np.int32)
    kind[:NEAR, :CELLS] = np.where(inside, np.where(qc >= kc, 1, 2), 0)
    kind[NEAR : NEAR + POOL] = 3
    col = np.arange(POOL) % HALF
    far = np.zeros((SLOTS - FAR_ROW, LANES), np.int32)
    shift = NEAR - FAR_ROW
    far[shift : shift + POOL, :POOL] = np.where(col[None] >= col[:, None], 1, 2)
    spread = np.zeros((LANES, WIDE), np.float32)
    spread[qr // 2 * HALF + qc // 2, q] = 1.0
    return kind, far, spread


def pooling():
    rows = SLOTS - FAR_ROW
    shift = NEAR - FAR_ROW
    token = np.arange(CELLS)
    out = np.zeros((2 * rows, ROWS), np.float32)
    for half in range(2):
        for i in range(shift):
            out[rows * half + i, FAR_ROW + i + OFFSET * half] = 1.0
        out[rows * half + shift + token // SIDE // 2 * HALF + token % SIDE // 2, token] = 0.25
    return out


def head_rows():
    lane = np.arange(2 * LANES) % LANES // HEAD_DIM
    return (lane[None] == np.arange(8)[:, None]).astype(np.float32)


def table_lines(tables):
    heads = tables.shape[0]
    fine = tables[:, : SPAN * SPAN].reshape(heads, SPAN, SPAN)[:, ::-1, ::-1]
    far = tables[:, SPAN * SPAN :].reshape(heads, FAR_SPAN, FAR_SPAN)

    def lines(part, pitch, lanes, centre):
        reach = part.shape[1] // 2
        right = jnp.pad(part[:, :, reach:], ((0, 0), (0, 0), (0, pitch - reach - 1)))
        left = jnp.pad(part[:, :, :reach], ((0, 0), (0, 0), (pitch - reach, 0)))
        start = centre - pitch * reach
        size = pitch * part.shape[1]
        right = jnp.pad(right.reshape(heads, size), ((0, 0), (start, lanes - start - size)))
        start = start - pitch
        left = jnp.pad(left.reshape(heads, size), ((0, 0), (start, lanes - start - size)))
        return right, left

    both = lines(fine, SIDE, LINE, CENTRE) + lines(far, HALF, LANES, FAR_CENTRE)
    return jnp.concatenate(both, axis=1)


def table_from_lines(right, left, far_right, far_left):
    heads = right.shape[0]

    def part(right, left, count, pitch, centre):
        reach = count // 2
        start = centre - pitch * reach
        size = pitch * count
        right = right[:, start : start + size].reshape(heads, count, pitch)[:, :, : reach + 1]
        start = start - pitch
        left = left[:, start : start + size].reshape(heads, count, pitch)[:, :, pitch - reach :]
        return jnp.concatenate([left, right], axis=2)

    fine = part(right, left, SPAN, SIDE, CENTRE)[:, ::-1, ::-1]
    far = part(far_right, far_left, FAR_SPAN, HALF, FAR_CENTRE)
    return jnp.concatenate([fine.reshape(heads, -1), far.reshape(heads, -1)], axis=1)


def spread_kernel(line_ref, kind_ref, far_kind_ref, spread_ref, out_ref):
    kind = kind_ref[...]
    far_kind = far_kind_ref[...]
    tiles = FAR_ROW // 8 + 1
    down = OFFSET // 8
    near_kind = kind[: 8 * tiles]
    lower = lax.broadcasted_iota(jnp.int32, (8, WIDE), 1) >= TOP
    shift = FAR_CENTRE + NEAR - FAR_ROW
    far_tiles = far_kind_ref.shape[0] // 8

    def stacked(part, tiles, centre, lanes):
        size = part.shape[1]
        base = pltpu.roll(jnp.broadcast_to(part, (8, size)), 0, 1, stride=1, stride_axis=0)
        return [pltpu.roll(base, (8 * t - centre) % size, 1)[:, :lanes] for t in range(tiles)]

    for h in range(GROUP):
        line = line_ref[0, h : h + 1]
        sides = []
        for start in (0, LINE):
            rolled = stacked(line[:, start : start + LINE], tiles + down, CENTRE, WIDE)
            sides.append(
                jnp.concatenate(
                    [jnp.where(lower, rolled[t + down], rolled[t]) for t in range(tiles)], axis=0
                )
            )
        fine = jnp.where(near_kind == 1, sides[0], jnp.where(near_kind == 2, sides[1], -1e9))
        far_line = line[:, 2 * LINE :]
        far_right = jnp.concatenate(stacked(far_line[:, :LANES], far_tiles, shift, LANES), axis=0)
        far_left = jnp.concatenate(stacked(far_line[:, LANES:], far_tiles, shift, LANES), axis=0)
        far = jnp.where(far_kind == 1, far_right, jnp.where(far_kind == 2, far_left, 0.0))
        far = nn(far, spread_ref[...], precision=lax.Precision.HIGHEST)
        rest = jnp.concatenate(
            [fine[FAR_ROW:], jnp.full((SLOTS - 8 * tiles, WIDE), -1e9, F32)], axis=0
        )
        out_ref[h, :FAR_ROW] = fine[:FAR_ROW] * (1.0 / SCALE)
        out_ref[h, FAR_ROW:] = jnp.where(kind[FAR_ROW:] == 3, far, rest) * (1.0 / SCALE)


def spread_tables(lines):
    heads = lines.shape[0]
    constants = [jnp.asarray(v) for v in kinds()]
    lines = lines.reshape(heads // GROUP, GROUP, -1)
    return pl.pallas_call(
        spread_kernel,
        grid=(heads // GROUP,),
        in_specs=[pl.BlockSpec((1,) + lines.shape[1:], lambda g: (g, 0, 0))]
        + [pl.BlockSpec(v.shape, lambda g: (0, 0)) for v in constants],
        out_specs=pl.BlockSpec((GROUP, SLOTS, WIDE), lambda g: (g, 0, 0)),
        out_shape=pltpu.HBM((heads, SLOTS, WIDE), F32),
        compiler_params=params(16),
        cost_estimate=cost(7),
        name="spread_tables",
    )(lines, *constants)


def unskew(tiles, lanes, centre):
    count = lanes // LANES
    wide = tiles[0].shape[1] // LANES
    zero = jnp.zeros((8, LANES), F32)
    total = [zero] * count
    lane = lax.broadcasted_iota(jnp.int32, (8, LANES), 1)
    for t, tile in enumerate(tiles):
        shift = (centre - 8 * t) % lanes
        first, part = shift // LANES, shift % LANES
        pieces = [tile[:, LANES * i : LANES * i + LANES] for i in range(wide)]
        if part:
            pieces = [pltpu.roll(v, part, 1) for v in pieces]
            pieces = [
                jnp.where(lane < part, left, right)
                for left, right in zip([zero] + pieces, pieces + [zero])
            ]
        for i, v in enumerate(pieces):
            total[(first + i) % count] = total[(first + i) % count] + v
    total = jnp.concatenate(total, axis=1)
    row = lax.broadcasted_iota(jnp.int32, (8, lanes), 0)
    out = jnp.where(row == 0, total, 0.0)
    for s in range(1, 8):
        out = out + jnp.where(row == s, pltpu.roll(total, lanes - s, 1), 0.0)
    return jnp.sum(out, axis=0, keepdims=True)


def collect(grad, side, kind_ref, far_kind_ref, spread_ref):
    tiles = FAR_ROW // 8 + 1
    down = OFFSET // 8
    part = jnp.where(kind_ref[: 8 * tiles] == side, grad[: 8 * tiles], 0.0)
    lower = lax.broadcasted_iota(jnp.int32, (8, WIDE), 1) >= TOP
    rows = [part[8 * t : 8 * t + 8] for t in range(tiles)]
    zero = jnp.zeros((8, WIDE), F32)
    both = [
        jnp.where(lower, low, high)
        for high, low in zip(rows + [zero] * down, [zero] * down + rows)
    ]
    far = grad[FAR_ROW:]
    high = far.astype(BF)
    rest = far - high.astype(F32)
    middle = rest.astype(BF)
    low = (rest - middle.astype(F32)).astype(BF)
    count = far.shape[0]
    far = nt(jnp.concatenate([high, middle, low], axis=0), spread_ref[...].astype(BF))
    far = far[:count] + far[count : 2 * count] + far[2 * count :]
    far = jnp.where(far_kind_ref[...] == side, far, 0.0)
    shift = FAR_CENTRE + NEAR - FAR_ROW
    far = [far[8 * t : 8 * t + 8] for t in range(count // 8)]
    return unskew(both, LINE, CENTRE), unskew(far, LANES, shift)


def norm_parts(stream):
    center = stream - jnp.mean(stream, axis=-1, keepdims=True)
    spread = jnp.mean(center * center, axis=-1, keepdims=True)
    rate = lax.rsqrt(spread + 1e-05)
    return center * rate, rate


def norm_back(unit, rate, gain, grad):
    inner = grad * gain
    mean = jnp.mean(inner, axis=-1, keepdims=True)
    along = jnp.mean(inner * unit, axis=-1, keepdims=True)
    return rate * (inner - mean - unit * along)


def tall(v):
    return jnp.concatenate([v, jnp.zeros((WIDE - v.shape[0], v.shape[1]), v.dtype)], axis=0)


def with_ones(v):
    return jnp.concatenate([v.T, jnp.ones((16, v.shape[0]), v.dtype)], axis=0)


def row_sum(v):
    return jnp.sum(v, axis=0, keepdims=True)


def prepare_kernel(core_ref, tokens_ref, cot_ref, x_ref, g_ref):
    images = x_ref.shape[0]
    for i in range(images):
        start = CELLS * i
        low = start // 16 * 16
        keep = lax.broadcasted_iota(jnp.int32, (ROWS, 1), 0) < CELLS
        for ref, out in ((tokens_ref, x_ref), (cot_ref, g_ref)):
            span = min(ROWS + 16, ref.shape[0] - low)
            v = ref[low : low + span].astype(F32)[start - low :]
            if v.shape[0] < ROWS:
                v = jnp.concatenate([v, jnp.zeros((ROWS - v.shape[0], v.shape[1]), F32)], axis=0)
            out[i] = jnp.where(keep, v[:ROWS], 0.0).astype(BF)


def prepare(tokens, cotangent, core):
    rows, width = cotangent.shape
    images = rows // CELLS
    padded = jax.ShapeDtypeStruct((images, ROWS, width), BF)
    whole = lambda shape: pl.BlockSpec(shape, lambda s, core: (0,) * len(shape))
    return pl.pallas_call(
        prepare_kernel,
        grid_spec=pltpu.PrefetchScalarGridSpec(
            num_scalar_prefetch=1,
            grid=(1,),
            in_specs=[
                pl.BlockSpec((rows, width), lambda s, core: (core[0], 0)),
                whole((rows, width)),
            ],
            out_specs=[whole(padded.shape)] * 2,
        ),
        out_shape=[padded] * 2,
        compiler_params=params(24),
        cost_estimate=cost(4),
        name="prepare",
    )(core, tokens, cotangent)


def shard_kernel(input_ref, output_t_ref, expand_t_ref, shrink_ref, out_ref):
    pack = jnp.concatenate([input_ref[t] for t in range(3)] + [output_t_ref[...]], axis=1)
    feed_part = jnp.concatenate([expand_t_ref[...], shrink_ref[...]], axis=1)
    out_ref[...] = jnp.concatenate([pack, feed_part], axis=0).astype(BF)


def shard(input_weight, output_t, expand_t, shrink):
    rows = output_t.shape[0] + shrink.shape[0]
    return pl.pallas_call(
        shard_kernel,
        out_shape=jax.ShapeDtypeStruct((rows, 2 * shrink.shape[1]), BF),
        compiler_params=params(60),
        cost_estimate=cost(1),
        name="shard",
    )(input_weight, output_t, expand_t, shrink)


def update_kernel(grad_ref, *refs):
    half = refs[0].shape[2]
    ins, outs = refs[:8], refs[8:]
    for t in range(3):
        grad = grad_ref[:, half * t : half * t + half]
        new = adamw(ins[0][t], grad, ins[1][t], ins[2][t], ins[3][t], 0.06, 0.05)
        for ref, value in zip(outs[:5], new + (new[0].astype(BF),)):
            ref[t] = value
    grad = grad_ref[:, 3 * half :]
    new = adamw(ins[4][...], grad, ins[5][...], ins[6][...], ins[7][...], 0.3, 0.05)
    for ref, value in zip(outs[5:], new + (new[0].astype(BF),)):
        ref[...] = value


def update(grad, inputs, outputs_t):
    shapes = []
    for v in (inputs[0], outputs_t[0]):
        shapes += [jax.ShapeDtypeStruct(v.shape, F32)] * 4 + [jax.ShapeDtypeStruct(v.shape, BF)]
    return pl.pallas_call(
        update_kernel,
        out_shape=shapes,
        compiler_params=params(16),
        cost_estimate=cost(1),
        name="update",
    )(grad, *inputs, *outputs_t)


def lanes_of(g, size=LANES):
    return pl.ds(pl.multiple_of(g * size, size), size)


def rows_of(g, h, size):
    return pl.ds(pl.multiple_of((g * GROUP + h) * size, size), size)


def place_of(core_ref, a, size):
    away = core_ref[1] ^ a
    out = 0
    for stride, radix in phases(size):
        out = out * radix + ((away >> (stride.bit_length() - 1)) & (radix - 1))
    return out


def assemble(core_ref, near_ref, far_ref, raw_s, win_s, wo_s, wint_ref, wot_ref):
    blocks, rows = near_ref.shape[0], near_ref.shape[1]
    width = wot_ref.shape[0]
    half = width // 2
    core = core_ref[0]
    for a in range(blocks):
        place = place_of(core_ref, a, blocks)
        raw_s[core, rows * a : rows * a + rows] = near_ref[place].astype(F32)
        raw_s[1 - core, rows * a : rows * a + rows] = far_ref[place].astype(F32)
    for t in range(4):
        whole = jnp.concatenate(
            [raw_s[h, :, half * t : half * t + half] for h in range(2)], axis=1
        ).astype(BF)
        if t < 3:
            win_s[:, width * t : width * t + width] = whole
            wint_ref[width * t : width * t + width] = whole.T
        else:
            wot_ref[...] = whole
            wo_s[...] = whole.T


def by_half(top, bottom):
    parts = []
    for g in range(top.shape[1] // LANES):
        lanes = slice(LANES * g, LANES * g + LANES)
        parts += [top[:, lanes], bottom[:, lanes]]
    return jnp.concatenate(parts, axis=1)


def to_slots(mixed, pool):
    high, low = split(mixed)
    far = nn(pool, jnp.concatenate([high, low], axis=0))
    rows = SLOTS - FAR_ROW
    top = jnp.concatenate([mixed[:FAR_ROW], far[:rows]], axis=0).astype(BF)
    bottom = jnp.concatenate([mixed[OFFSET : OFFSET + FAR_ROW], far[rows:]], axis=0).astype(BF)
    width = mixed.shape[1] // 2
    return [by_half(top[:, :width], bottom[:, :width]), by_half(top[:, width:], bottom[:, width:])]


def from_slots(grads, pool_t):
    groups = grads[0].shape[1] // WIDE
    top, bottom = (
        jnp.concatenate(
            [
                grad[:, WIDE * g + LANES * i : WIDE * g + LANES * i + LANES]
                for grad in grads
                for g in range(groups)
            ],
            axis=1,
        )
        for i in range(2)
    )
    high, low = split(jnp.concatenate([top[FAR_ROW:], bottom[FAR_ROW:]], axis=0))
    out = nn(pool_t, jnp.concatenate([high, low], axis=0))
    zeros = lambda count: jnp.zeros((count, top.shape[1]), F32)
    return (
        out
        + jnp.concatenate([top[:FAR_ROW], zeros(ROWS - FAR_ROW)], axis=0)
        + jnp.concatenate(
            [zeros(OFFSET), bottom[:FAR_ROW], zeros(ROWS - FAR_ROW - OFFSET)], axis=0
        )
    )


def turned(slots_ref, target_ref):
    flat = slots_ref[...].T
    for g in range(flat.shape[0] // WIDE):
        for h in range(GROUP):
            for i in range(2):
                source = WIDE * g + LANES * i + HEAD_DIM * h
                target = 2 * HEAD_DIM * (GROUP * g + h) + HEAD_DIM * i
                target_ref[target : target + HEAD_DIM] = flat[source : source + HEAD_DIM]


def masked(source, heads_ref, target_ref):
    for h in range(GROUP):
        target_ref[SLOTS * h : SLOTS * h + SLOTS] = source * heads_ref[h : h + 1]


def sides_of_lanes(v, target_ref):
    lane = lax.broadcasted_iota(jnp.int32, v.shape, 1)
    zero = jnp.zeros_like(v)
    target_ref[:LANES] = jnp.where(lane < TOP, v, zero)
    target_ref[LANES:] = jnp.where(lane < TOP, zero, v)


def choose_half(pair):
    lane = lax.broadcasted_iota(jnp.int32, (HEAD_DIM, WIDE), 1)
    return jnp.where(lane < TOP, pair[:HEAD_DIM], pair[HEAD_DIM:])


HALVES = [slice(0, LANES), slice(LANES, WIDE)]


def forward_kernel(
    core_ref,
    keep_ref,
    near_ref,
    far_ref,
    x_ref,
    vec_ref,
    bias_ref,
    pool_ref,
    heads_ref,
    state_ref,
    att_ref,
    p_ref,
    q_ref,
    k_ref,
    v_ref,
    wint_ref,
    wot_ref,
    raw_s,
    win_s,
    wo_s,
    s_s,
    km_s,
    qb_s,
    vt_s,
    att_t,
    qt_s,
):
    step = pl.program_id(0)
    width = wot_ref.shape[0]
    groups = width // LANES

    @pl.when(step == 0)
    def _():
        assemble(core_ref, near_ref, far_ref, raw_s, win_s, wo_s, wint_ref, wot_ref)

    x = x_ref[...].reshape(PAIR * ROWS, width).astype(F32)
    ln = (norm_parts(x)[0] * vec_ref[0:1] + vec_ref[1:2]).astype(BF)
    mixed = nn(ln, win_s[...])
    for b in range(PAIR):
        own = mixed[ROWS * b : ROWS * b + ROWS]
        query = (own[:, :width] + vec_ref[2:3]).astype(BF)
        q_ref[b] = query
        qt_s[b] = tall(query).T
        shift = jnp.concatenate([jnp.zeros((1, width), F32), vec_ref[3:4]], axis=1)
        k_ref[b], v_ref[b] = to_slots(own[:, width:] + shift, pool_ref[...])
        turned(v_ref.at[b], vt_s.at[b])

    def products(g):
        for b in range(PAIR):
            slot = g % 2 * PAIR + b
            masked(k_ref[b, :, WIDE * g : WIDE * g + WIDE], heads_ref, km_s.at[slot])
            sides_of_lanes(qt_s[b, LANES * g : LANES * g + LANES], qb_s.at[slot])
            s_s[slot] = nn(km_s[slot], qb_s[slot])

    products(0)
    for g in range(groups):
        if g + 1 < groups:
            products(g + 1)
        for b in range(PAIR):
            for h in range(GROUP):
                n = g * GROUP + h
                slots = slice(SLOTS * h, SLOTS * h + SLOTS)
                for half in HALVES:
                    scores = s_s[g % 2 * PAIR + b, slots, half] + bias_ref[n, :, half]
                    top = jnp.max(scores, axis=0, keepdims=True)
                    weights = jnp.exp2((scores - top) * TO_LOG2)
                    total = jnp.sum(weights, axis=0, keepdims=True)
                    p_ref[b, n, :, half] = (weights * (1.0 / total)).astype(BF)
                both = nn(vt_s[b, 2 * HEAD_DIM * n : 2 * HEAD_DIM * (n + 1)], p_ref[b, n])
                att_t[b, HEAD_DIM * n : HEAD_DIM * (n + 1)] = choose_half(both).astype(BF)

    for b in range(PAIR):
        att_ref[b] = att_t[b].T[:ROWS]
    branch = nn(att_ref[...].reshape(PAIR * ROWS, width), wo_s[...]) + vec_ref[4:5]
    for b in range(PAIR):
        scale = DROP_SCALE * keep_ref[step * PAIR + b, 0].astype(F32)
        own = branch[ROWS * b : ROWS * b + ROWS]
        state_ref[b] = x_ref[b].astype(F32) + scale * own


def attend_forward(core, flags, near, far, x, vectors, bias):
    images, _, width = x.shape
    fixed = lambda shape: pl.BlockSpec(shape, lambda s, *_: (0,) * len(shape))
    pair = lambda *shape: pl.BlockSpec((PAIR,) + shape, lambda s, *_: (s,) + (0,) * len(shape))
    pool = np.concatenate([pooling()] * 2, axis=1)
    shapes = [
        ((images, ROWS, width), F32),
        ((images, ROWS, width), BF),
        ((images,) + bias.shape, BF),
        ((images, ROWS, width), BF),
        ((images, SLOTS, 2 * width), BF),
        ((images, SLOTS, 2 * width), BF),
        ((3 * width, width), BF),
        ((width, width), BF),
    ]
    return pl.pallas_call(
        forward_kernel,
        grid_spec=pltpu.PrefetchScalarGridSpec(
            num_scalar_prefetch=2,
            grid=(images // PAIR,),
            in_specs=[
                fixed(near.shape),
                fixed(far.shape),
                pair(ROWS, width),
                fixed(vectors.shape),
                fixed(bias.shape),
                fixed(pool.shape),
                fixed((8, WIDE)),
            ],
            out_specs=[
                pair(ROWS, width),
                pair(ROWS, width),
                pair(*bias.shape),
                pair(ROWS, width),
                pair(SLOTS, 2 * width),
                pair(SLOTS, 2 * width),
                fixed((3 * width, width)),
                fixed((width, width)),
            ],
            scratch_shapes=[
                pltpu.VMEM((2, width, 2 * width), F32),
                pltpu.VMEM((width, 3 * width), BF),
                pltpu.VMEM((width, width), BF),
                pltpu.VMEM((2 * PAIR, GROUP * SLOTS, WIDE), F32),
                pltpu.VMEM((2 * PAIR, GROUP * SLOTS, WIDE), BF),
                pltpu.VMEM((2 * PAIR, WIDE, WIDE), BF),
                pltpu.VMEM((PAIR, 2 * width, SLOTS), BF),
                pltpu.VMEM((PAIR, width, WIDE), BF),
                pltpu.VMEM((PAIR, width, WIDE), BF),
            ],
        ),
        out_shape=[pltpu.HBM(s, d) for s, d in shapes],
        compiler_params=params(60),
        cost_estimate=cost(25),
        name="attend_forward",
    )(
        core,
        flags,
        near,
        far,
        x,
        vectors,
        bias,
        jnp.asarray(pool, BF),
        jnp.asarray(head_rows(), BF),
    )


def feed_kernel(
    core_ref,
    keep_ref,
    state_ref,
    g_ref,
    att_ref,
    ff0_ref,
    ff1_ref,
    wot_ref,
    vec_ref,
    fb_ref,
    result_ref,
    grad_ref,
    dout_ref,
    dff0_ref,
    dff1_ref,
    dwot_ref,
    rows_ref,
    ws_s,
    we_s,
    ff0_s,
    ff1_s,
):
    step = pl.program_id(0)
    last = pl.num_programs(0) - 1
    width = wot_ref.shape[0]
    chunks = 2 * dff0_ref.shape[0] // width
    blocks, block = ff0_ref.shape[0], ff0_ref.shape[1]
    count = MANY * ROWS

    @pl.when(step == 0)
    def _():
        ws_s[...] = jnp.zeros_like(ws_s)
        we_s[...] = jnp.zeros_like(we_s)
        dwot_ref[...] = jnp.zeros_like(dwot_ref)
        rows_ref[...] = jnp.zeros_like(rows_ref)
        for a in range(blocks):
            place = place_of(core_ref, a, blocks)
            here = slice(block * a, block * a + block)
            ff0_s[here] = ff0_ref[place]
            ff1_s[here] = ff1_ref[place]

    def column(which):
        row = lax.broadcasted_iota(jnp.int32, (count, 1), 0)
        out = keep_ref[step * MANY, which].astype(F32)
        for b in range(1, MANY):
            out = jnp.where(row < b * ROWS, out, keep_ref[step * MANY + b, which].astype(F32))
        return jnp.broadcast_to(out * DROP_SCALE, (count, 1))

    state = state_ref[...].reshape(count, width)
    upstream = g_ref[...].reshape(count, width).astype(F32)
    unit, rate = norm_parts(state)
    gain = vec_ref[5:6]
    ln = (unit * gain + vec_ref[6:7]).astype(BF)
    keep = column(1)
    scaled = keep * upstream
    signal = scaled.astype(BF)
    ln_t = with_ones(ln)
    signal_t = signal.T

    out = jnp.zeros((count, width), F32)
    grad_ln = jnp.zeros((count, width), F32)
    for c in range(chunks):
        piece = slice(width * c, width * c + width)
        ff_s = ff0_s if c < chunks // 2 else ff1_s
        here = slice(width * (c % (chunks // 2)), width * (c % (chunks // 2)) + width)
        we, ws = ff_s[here, :width], ff_s[here, width:]
        row = (c + core_ref[0] * (chunks // 2)) % chunks
        pre = nt(ln, we) + fb_ref[pl.ds(row, 1)]
        part = 0.5 * (1.0 + lax.erf(pre * np.float32(0.5**0.5)))
        act = (pre * part).astype(BF)
        slope = part + pre * (jnp.exp(-0.5 * pre * pre) * np.float32((2 * np.pi) ** -0.5))
        grad_pre = (nt(signal, ws) * slope).astype(BF)
        out = out + nn(act, ws)
        grad_ln = grad_ln + nn(grad_pre, we)
        ws_s[:, piece] += nn(signal_t, act)
        part = nn(ln_t, grad_pre)
        we_s[:, piece] += part[:width]
        rows_ref[pl.ds(4 + row, 1)] += part[width : width + 1]

    result = state + keep * (out + vec_ref[7:8])
    grad_state = upstream + norm_back(unit, rate, gain, grad_ln)
    for b in range(MANY):
        result_ref[CELLS * b : CELLS * b + CELLS] = result[ROWS * b : ROWS * b + CELLS]
    grad_ref[...] = grad_state.reshape(MANY, ROWS, width)
    scaled_one = column(0) * grad_state
    one = scaled_one.astype(BF)
    dout_ref[...] = nn(one, wot_ref[...]).astype(BF).reshape(MANY, ROWS, width)
    dwot_ref[...] += nn(one.T, att_ref[...].reshape(count, width))
    rows_ref[0:1] += row_sum(scaled_one)
    rows_ref[1:2] += row_sum(grad_ln * unit)
    rows_ref[2:3] += row_sum(grad_ln)
    rows_ref[3:4] += row_sum(scaled)

    @pl.when(step == last)
    def _():
        half = chunks // 2
        for c in range(chunks):
            piece = slice(width * c, width * c + width)
            here = slice(width * (c % half), width * (c % half) + width)
            target = dff0_ref if c < half else dff1_ref
            target[here, :width] = we_s[:, piece].astype(BF).T
            target[here, width:] = ws_s[:, piece].astype(BF).T


def feed(core, flags, state, g, att, ff0, ff1, wot, vectors, fb):
    images, _, width = state.shape
    hidden = 2 * ff0.shape[0] * ff0.shape[1]
    fixed = lambda shape: pl.BlockSpec(shape, lambda s, *_: (0,) * len(shape))
    pair = lambda *shape: pl.BlockSpec((MANY,) + shape, lambda s, *_: (s,) + (0,) * len(shape))
    shapes = [
        ((images * CELLS, width), F32),
        ((images, ROWS, width), F32),
        ((images, ROWS, width), BF),
        ((hidden // 2, 2 * width), BF),
        ((hidden // 2, 2 * width), BF),
        ((width, width), F32),
        ((8, width), F32),
    ]
    return pl.pallas_call(
        feed_kernel,
        grid_spec=pltpu.PrefetchScalarGridSpec(
            num_scalar_prefetch=2,
            grid=(images // MANY,),
            in_specs=[
                pair(ROWS, width),
                pair(ROWS, width),
                pair(ROWS, width),
                fixed(ff0.shape),
                fixed(ff1.shape),
                fixed((width, width)),
                fixed(vectors.shape),
                fixed(fb.shape),
            ],
            out_specs=[
                pl.BlockSpec((MANY * CELLS, width), lambda s, *_: (s, 0)),
                pair(ROWS, width),
                pair(ROWS, width),
                fixed((hidden // 2, 2 * width)),
                fixed((hidden // 2, 2 * width)),
                fixed((width, width)),
                fixed((8, width)),
            ],
            scratch_shapes=[
                pltpu.VMEM((width, hidden), F32),
                pltpu.VMEM((width, hidden), F32),
                pltpu.VMEM((hidden // 2, 2 * width), BF),
                pltpu.VMEM((hidden // 2, 2 * width), BF),
            ],
        ),
        out_shape=[jax.ShapeDtypeStruct(s, d) for s, d in shapes],
        compiler_params=params(56),
        cost_estimate=cost(35),
        name="feed",
    )(core, flags, state, g, att, ff0, ff1, wot, vectors, fb)


def add_kernel(one_ref, two_ref, out_ref):
    out_ref[...] = one_ref[...] + two_ref[...]


def add(one, two):
    rows, lanes = one.shape
    block = pl.BlockSpec((rows // 2, lanes), lambda s: (s, 0))
    return pl.pallas_call(
        add_kernel,
        grid=(2,),
        in_specs=[block, block],
        out_specs=block,
        out_shape=jax.ShapeDtypeStruct(one.shape, one.dtype),
        compiler_params=params(16),
        cost_estimate=cost(1.5),
        name="add",
    )(one, two)


def diagonal(whole):
    lane = lax.broadcasted_iota(jnp.int32, (SLOTS, WIDE), 1) % LANES
    out = whole[SLOTS * (GROUP - 1) :]
    for h in reversed(range(GROUP - 1)):
        out = jnp.where(lane < HEAD_DIM * (h + 1), whole[SLOTS * h : SLOTS * h + SLOTS], out)
    return out


def sides_of_rows(v, target_ref):
    row = lax.broadcasted_iota(jnp.int32, v.shape, 0)
    zero = jnp.zeros_like(v)
    target_ref[:, :LANES] = jnp.where(row < TOP, v, zero)
    target_ref[:, LANES:] = jnp.where(row < TOP, zero, v)


def small_rows(lines_ref, vector_rows, core):
    groups = lines_ref.shape[0]
    heads = groups * GROUP
    lanes = 2 * LINE
    first, rest = [], []
    for i in range(heads):
        g, h = i // GROUP, i % GROUP
        pair = [lines_ref[g, side, h : h + 1] for side in range(2)]
        first.append(jnp.concatenate([v[:, :LINE] for v in pair], axis=1))
        rest += [v[:, LINE:] for v in pair]
    per_row = lanes // LANES
    rest = [jnp.concatenate(rest[i : i + per_row], axis=1) for i in range(0, len(rest), per_row)]
    sums = [
        jnp.concatenate([vector_rows[i : i + 1], vector_rows[i + 1 : i + 2]], axis=1)
        for i in range(0, vector_rows.shape[0], 2)
    ]
    halves = [
        jnp.concatenate(
            [
                row
                for rows in (first, rest, sums)
                for row in rows[len(rows) // 2 * c : len(rows) // 2 * (c + 1)]
            ],
            axis=0,
        )
        for c in range(2)
    ]
    return jnp.where(core == 0, halves[0], halves[1])


def backward_kernel(
    core_ref,
    x_ref,
    grad_ref,
    dout_ref,
    q_ref,
    k_ref,
    v_ref,
    p_ref,
    wint_ref,
    vec_ref,
    dwot_ref,
    rows_two_ref,
    pool_t_ref,
    heads_ref,
    kind_ref,
    far_kind_ref,
    spread_ref,
    igrad_ref,
    near_ref,
    far_ref,
    dwin_s,
    rows_s,
    lines_s,
    dense0_s,
    dense1_s,
    dense2_s,
    dense3_s,
    k_t,
    raw_qt,
    raw_k,
    raw_v,
    mixed_s,
    whole_s,
    d_s,
    ds_s,
    vm_s,
    db_s,
    qr_s,
    dr_s,
):
    phase, step = pl.program_id(0), pl.program_id(1)
    width = wint_ref.shape[1]
    groups = width // LANES
    now, before = phase % 2, (phase + 1) % 2
    dense_refs = (dense0_s, dense1_s, dense2_s, dense3_s)

    def collect_before():
        g = jnp.maximum(phase - 1, 0)
        for h in range(GROUP):
            fine, far = collect(
                dense_refs[h][before], step + 1, kind_ref, far_kind_ref, spread_ref
            )
            lines_s[g, step, h : h + 1, :LINE] = fine
            lines_s[g, step, h : h + 1, LINE:] = far

    @pl.when((phase == 0) & (step == 0))
    def _():
        dwin_s[...] = jnp.zeros_like(dwin_s)
        rows_s[...] = jnp.zeros_like(rows_s)
        for ref in dense_refs:
            ref[...] = jnp.zeros_like(ref)

    @pl.when((phase > 0) & (phase < groups) & (step == 0))
    def _():
        for ref in dense_refs:
            ref[now] = jnp.zeros(ref.shape[1:], F32)

    @pl.when((phase > 0) & (phase < groups))
    def _():
        collect_before()

    @pl.when(phase < groups)
    def _():
        def products(i):
            for b in range(PAIR):
                n = i * PAIR + b
                keys, values = k_ref[n], v_ref[n]
                flat = keys.T
                for h in range(GROUP):
                    for side in range(2):
                        source = LANES * side + HEAD_DIM * h
                        target = HEAD_DIM * (2 * h + side)
                        k_t[i * PAIR + b, target : target + HEAD_DIM] = flat[source : source + HEAD_DIM]
                masked(values, heads_ref, vm_s.at[i * PAIR + b])
                dout = tall(dout_ref[n])
                sides_of_lanes(dout.T, db_s.at[i * PAIR + b])
                d_s[i * PAIR + b] = nn(vm_s[i * PAIR + b], db_s[i * PAIR + b])
                sides_of_rows(tall(q_ref[n]), qr_s.at[i * PAIR + b])
                sides_of_rows(dout, dr_s.at[i * PAIR + b])

        def attend(i):
            for h in range(GROUP):
                slots = slice(SLOTS * h, SLOTS * h + SLOTS)
                for half in HALVES:
                    dense = dense_refs[h][now, :, half]
                    for b in range(PAIR):
                        probs = p_ref[i * PAIR + b, h, :, half].astype(F32)
                        grad_probs = d_s[i * PAIR + b, slots, half]
                        along = jnp.sum(probs * grad_probs, axis=0, keepdims=True)
                        grad_scores = (probs * (grad_probs - along)).astype(BF)
                        ds_s[i * PAIR + b, slots, half] = grad_scores
                        dense = dense + grad_scores.astype(F32)
                    dense_refs[h][now, :, half] = dense
                for b in range(PAIR):
                    both = nn(k_t[i * PAIR + b, 2 * HEAD_DIM * h : 2 * HEAD_DIM * (h + 1)], ds_s[i * PAIR + b, slots])
                    raw_qt[step * MANY + i * PAIR + b, rows_of(phase, h, HEAD_DIM), :] = (
                        choose_half(both) * SCALE
                    ).astype(BF)
            wide = lanes_of(phase, WIDE)
            for b in range(PAIR):
                n = step * MANY + i * PAIR + b
                probs = p_ref[i * PAIR + b].reshape(GROUP * SLOTS, WIDE)
                raw_v[n, :, wide] = diagonal(nn(probs, dr_s[i * PAIR + b]))
                raw_k[n, :, wide] = diagonal(nn(ds_s[i * PAIR + b], qr_s[i * PAIR + b])) * SCALE

        products(0)
        for i in range(MANY // PAIR):
            if i + 1 < MANY // PAIR:
                products(i + 1)
            attend(i)

    @pl.when(phase == groups)
    def _():
        collect_before()
        gain = vec_ref[0:1]
        for i in range(MANY // PAIR):
            for b in range(PAIR):
                n = step * MANY + i * PAIR + b
                rows = slice(ROWS * b, ROWS * b + ROWS)
                mixed_s[rows, :width] = raw_qt[n].T[:ROWS]
                mixed_s[rows, width:] = from_slots([raw_k[n], raw_v[n]], pool_t_ref[...]).astype(BF)
            mixed = mixed_s[...]
            own = slice(PAIR * i, PAIR * i + PAIR)
            x = x_ref[own].reshape(PAIR * ROWS, width).astype(F32)
            unit, rate = norm_parts(x)
            ln = (unit * gain + vec_ref[1:2]).astype(BF)
            part = nn(with_ones(ln), mixed)
            dwin_s[...] += part[:width]
            sums = part[width:]
            grad_ln = nn(mixed, wint_ref[...])
            out = grad_ref[own].reshape(PAIR * ROWS, width) + norm_back(unit, rate, gain, grad_ln)
            for b in range(PAIR):
                n = PAIR * i + b
                igrad_ref[CELLS * n : CELLS * n + CELLS] = out[ROWS * b : ROWS * b + CELLS]
            rows_s[0:1] += row_sum(grad_ln * unit)
            rows_s[1:2] += row_sum(grad_ln)
            rows_s[2:3] += sums[:1, :width]
            rows_s[3:4] += sums[:1, 2 * width :]

    @pl.when((phase == groups) & (step == pl.num_programs(1) - 1))
    def _():
        rows = near_ref.shape[1]
        blocks = width // rows
        half = width // 2
        core = core_ref[0]
        for h in range(2):
            parts = [
                dwin_s[:, width * t + half * h : width * t + half * h + half] for t in range(3)
            ] + [dwot_ref[:, half * h : half * h + half]]
            whole_s[h] = jnp.concatenate(parts, axis=1)
        for a in range(blocks):
            place = place_of(core_ref, a, blocks)
            here = slice(rows * a, rows * a + rows)
            near_ref[place] = whole_s[core, here].astype(BF)
            far_ref[place] = whole_s[1 - core, here].astype(BF)
        sums = jnp.concatenate([rows_s[:4], rows_two_ref[...]], axis=0)
        extra = near_ref.shape[0] - blocks
        for ref, which in ((near_ref, core), (far_ref, 1 - core)):
            small = small_rows(lines_s, sums, which)
            pad = jnp.zeros((extra * rows - small.shape[0], small.shape[1]), F32)
            small = jnp.concatenate([small, pad], axis=0) if pad.shape[0] else small
            for i in range(extra):
                ref[blocks + i] = small[rows * i : rows * i + rows].astype(BF)


SMALL = 11


def attend_backward(
    core, pack_shape, x, grad, dout, q, k, v, probs, win_t, vectors, dwot, rows_two
):
    images, _, width = x.shape
    groups = width // LANES
    end = images // MANY - 1
    fixed = lambda shape: pl.BlockSpec(shape, lambda p, s, *_: (0,) * len(shape))
    late = lambda *shape: pl.BlockSpec(
        (MANY,) + shape,
        lambda p, s, *_: (jnp.where(p == groups, s, 0),) + (0,) * len(shape),
    )

    def early(shape, axis):
        def where(p, s, *_):
            place = [jnp.where(p == groups, end, s)] + [0] * len(shape)
            place[axis] = jnp.minimum(p, groups - 1)
            return tuple(place)

        return pl.BlockSpec((MANY,) + shape, where)

    blocks, rows, lanes = pack_shape
    pack_shape = (blocks + -(-SMALL // rows), rows, lanes)
    pool_t = np.concatenate([pooling().T] * 2, axis=1)
    tables = kinds()
    shapes = [((images * CELLS, width), F32), (pack_shape, BF), (pack_shape, BF)]
    stack = (MANY, GROUP * SLOTS, WIDE)
    square = (MANY, WIDE, WIDE)
    return pl.pallas_call(
        backward_kernel,
        grid_spec=pltpu.PrefetchScalarGridSpec(
            num_scalar_prefetch=1,
            grid=(groups + 1, images // MANY),
            in_specs=[
                late(ROWS, width),
                late(ROWS, width),
                early((ROWS, LANES), 2),
                early((ROWS, LANES), 2),
                early((SLOTS, WIDE), 2),
                early((SLOTS, WIDE), 2),
                early((GROUP, SLOTS, WIDE), 1),
                fixed(win_t.shape),
                fixed(vectors.shape),
                fixed(dwot.shape),
                fixed(rows_two.shape),
                fixed(pool_t.shape),
                fixed((8, WIDE)),
            ]
            + [fixed(v.shape) for v in tables],
            out_specs=[
                pl.BlockSpec(
                    (MANY * CELLS, width), lambda p, s, *_: (jnp.where(p == groups, s, 0), 0)
                ),
                fixed(pack_shape),
                fixed(pack_shape),
            ],
            scratch_shapes=[
                pltpu.VMEM((width, 3 * width), F32),
                pltpu.VMEM((8, width), F32),
                pltpu.VMEM((groups, 2, GROUP, LINE + LANES), F32),
                pltpu.VMEM((2, SLOTS, WIDE), F32),
                pltpu.VMEM((2, SLOTS, WIDE), F32),
                pltpu.VMEM((2, SLOTS, WIDE), F32),
                pltpu.VMEM((2, SLOTS, WIDE), F32),
                pltpu.VMEM((MANY, WIDE, SLOTS), BF),
                pltpu.VMEM((images, width, WIDE), BF),
                pltpu.VMEM((images, SLOTS, 2 * width), F32),
                pltpu.VMEM((images, SLOTS, 2 * width), F32),
                pltpu.VMEM((PAIR * ROWS, 3 * width), BF),
                pltpu.VMEM((2, width, 2 * width), F32),
                pltpu.VMEM(stack, F32),
                pltpu.VMEM(stack, BF),
                pltpu.VMEM(stack, BF),
                pltpu.VMEM(square, BF),
                pltpu.VMEM(square, BF),
                pltpu.VMEM(square, BF),
            ],
        ),
        out_shape=[jax.ShapeDtypeStruct(s, d) for s, d in shapes],
        compiler_params=params(60),
        cost_estimate=cost(45),
        name="attend_backward",
    )(
        core,
        x,
        grad,
        dout,
        q,
        k,
        v,
        probs,
        win_t,
        vectors,
        dwot,
        rows_two,
        jnp.asarray(pool_t, BF),
        jnp.asarray(head_rows(), BF),
        *[jnp.asarray(v) for v in tables],
    )


def phases(size):
    out, stride = [], 1
    while stride < size:
        radix = 4 if size // stride % 4 == 0 else 2
        out.append((stride, radix))
        stride *= radix
    return out


def hop(v, stride, mask):
    return lax.ppermute(
        v, "dp", [(i, i ^ (mask * stride)) for i in range(lax.axis_size("dp"))]
    )


def meet(v, stride, radix):
    return jnp.stack([v] + [hop(v, stride, m) for m in range(1, radix)])


def swap(v):
    return lax.ppermute(v, "head", [(0, 1), (1, 0)])


def exchange(v):
    return lax.all_to_all(v, "dp", 0, 0)


def repeat(v, times):
    return jnp.broadcast_to(v[None], (times,) + v.shape)


def tree_sum(parts):
    while len(parts) > 1:
        parts = [parts[i] + parts[i + 1] for i in range(0, len(parts), 2)]
    return parts[0]


def reduce_parts(v, small):
    blocks, rows, lanes = v.shape
    v = v.reshape(blocks * rows, lanes)
    for stride, radix in phases(blocks):
        count = v.shape[0] // radix
        small = small.astype(BF)
        got = [
            hop(
                jnp.concatenate([v[count * m : count * m + count].astype(BF), small], axis=0),
                stride,
                m,
            ).astype(F32)
            for m in range(1, radix)
        ]
        v = tree_sum([v[:count]] + [g[:count] for g in got])
        small = tree_sum([small.astype(F32)] + [g[count:] for g in got])
    return v, small


def by_core(core, near, far):
    return jnp.where(core == 0, near, far), jnp.where(core == 0, far, near)


def adamw(weight, grad, first, second, average, rate, decay):
    first = 0.9 * first + 0.1 * grad
    second = 0.999 * second + 0.001 * grad * grad
    fix_one = 1.0 - 0.9**STEP
    fix_two = 1.0 - 0.999**STEP
    weight = weight - rate * (
        first / fix_one / (jnp.sqrt(second / fix_two) + 1e-08) + decay * weight
    )
    average = 0.9 * average + 0.1 * weight
    return (weight, first, second, average)


def shards(
    tokens,
    keep,
    cotangent,
    input_weight,
    output_weight,
    expand_weight,
    shrink_weight,
    bias_tables,
    vectors,
    first_input,
    second_input,
    average_input,
    first_output,
    second_output,
    average_output,
    first_expand,
    second_expand,
    average_expand,
    first_shrink,
    second_shrink,
    average_shrink,
    first_tables,
    second_tables,
    average_tables,
    first_vectors,
    second_vectors,
    average_vectors,
):
    dp, head = lax.axis_size("dp"), lax.axis_size("head")
    core = lax.axis_index("head")
    width = vectors.shape[1]
    own_images = cotangent.shape[0] // CELLS
    rows = input_weight.shape[1]
    hidden = expand_weight.shape[1] * dp * head
    block = hidden // (dp * head)

    part = shard(input_weight, output_weight.T, expand_weight.T, shrink_weight)
    pick = jnp.stack([core, lax.axis_index("dp")]).astype(jnp.int32)
    tables = by_core(core, bias_tables, swap(bias_tables))
    lines = table_lines(jnp.concatenate(tables, axis=0))
    x, g = prepare(tokens, cotangent, pick)
    *high, low = reversed(phases(dp))
    for stride, radix in high:
        part = meet(part, stride, radix)
    lines, part, x, g = lax.optimization_barrier((lines, part, x, g))
    bias = spread_tables(lines)
    part = part.reshape(-1, *part.shape[-2:])
    pack0 = meet(part[:, :rows], *low)
    ff, pack0, bias = lax.optimization_barrier((part[:, rows:], pack0, bias))
    pack0 = pack0.reshape(dp, rows, 2 * width)
    pack1 = swap(pack0)
    ff_parts = [ff] + [hop(ff, low[0], m) for m in range(1, low[1])]
    flags = lax.dynamic_slice_in_dim(keep, core * own_images, own_images, 0)
    fb = vectors[8:].reshape(dp, head, block).swapaxes(0, 1).reshape(-1, width)

    state, att, probs, q, k, v, win_t, wot = attend_forward(
        pick, flags, pack0, pack1, x, vectors, bias
    )
    ff_parts, state = lax.optimization_barrier((ff_parts, state))
    ff0 = jnp.concatenate(ff_parts, axis=0)
    ff1 = swap(ff0)
    result, grad_state, dout, dff0, dff1, dwot, rows_two = feed(
        pick, flags, state, g, att, ff0, ff1, wot, vectors, fb
    )
    dff = add(dff0, swap(dff1)).reshape(dp, block, 2 * width)
    dff, dout = lax.optimization_barrier((dff, dout))
    dff = exchange(dff)
    input_grad, dpack0, dpack1 = attend_backward(
        pick,
        pack0.shape,
        x,
        grad_state,
        dout,
        q,
        k,
        v,
        probs,
        win_t,
        vectors,
        dwot,
        rows_two,
    )
    dff, dpack1 = lax.optimization_barrier((dff, dpack1))
    ff_grad = jnp.sum(dff.astype(F32), axis=0)

    dpack = dpack0.astype(F32) + swap(dpack1).astype(F32)
    small = dpack[dp:].reshape(-1, 2 * width)[: -(-SMALL // 8) * 8]
    pack_grad, small = reduce_parts(dpack[:dp], small)
    local_heads = bias_tables.shape[0]
    lines = small[:local_heads]
    far = small[local_heads : local_heads + local_heads // 3].reshape(local_heads, 2, LANES)
    table_grad = table_from_lines(lines[:, :LINE], lines[:, LINE:], far[:, 0], far[:, 1])
    own_vector = small[local_heads + local_heads // 3 : SMALL]
    vector_total = jnp.concatenate(by_core(core, own_vector, swap(own_vector)))
    vector_total = vector_total.reshape(vectors.shape)
    fb_total = vector_total[8:].reshape(head, dp, block).swapaxes(0, 1).reshape(-1, width)
    vector_total = jnp.concatenate([vector_total[:8], fb_total])

    new = update(
        pack_grad,
        (input_weight, first_input, second_input, average_input),
        (output_weight.T, first_output.T, second_output.T, average_output.T),
    )
    input_new, output_new = new[:5], [v.T for v in new[5:]]
    grad_expand = ff_grad[:, :width].T
    grad_shrink = ff_grad[:, width:]
    expand_new = adamw(
        expand_weight, grad_expand, first_expand, second_expand, average_expand, 0.06, 0.05
    )
    shrink_new = adamw(
        shrink_weight, grad_shrink, first_shrink, second_shrink, average_shrink, 0.06, 0.05
    )
    tables_new = adamw(
        bias_tables, table_grad, first_tables, second_tables, average_tables, 1.0, 0.0
    )
    vectors_new = adamw(
        vectors, vector_total, first_vectors, second_vectors, average_vectors, 0.6, 0.0
    )
    return (
        result,
        input_grad,
        *input_new,
        *output_new,
        *expand_new,
        expand_new[0].astype(BF),
        *shrink_new,
        shrink_new[0].astype(BF),
        *tables_new,
        *vectors_new,
    )


def solution(mesh):
    both = P(("dp", "head"), None)
    inputs = P(None, "dp", "head")
    output = P("head", "dp")
    expand = P(None, ("dp", "head"))
    tables = P("head", None)
    in_specs = (
        (P("dp", None), P("dp", None), both, inputs, output, expand, both, tables, P())
        + (inputs,) * 3
        + (output,) * 3
        + (expand,) * 3
        + (both,) * 3
        + (tables,) * 3
        + (P(),) * 3
    )
    out_specs = (
        (both, both)
        + (inputs,) * 5
        + (output,) * 5
        + (expand,) * 5
        + (both,) * 5
        + (tables,) * 4
        + (P(),) * 4
    )
    return jax.shard_map(shards, mesh=mesh, in_specs=in_specs, out_specs=out_specs, check_vma=False)
```

```python
from functools import partial

import jax
import jax.numpy as jnp
import numpy as np
from jax import lax
from jax.experimental import pallas as pl
from jax.experimental.pallas import tpu as pltpu
from jax.sharding import PartitionSpec as P

HEAD_DIM = 32
SIDE = 14
WINDOW = 7
FINE = 13
STEP = 10
DROP_SCALE = 1.25

CELLS = SIDE * SIDE
HALF = SIDE // 2
POOL = HALF * HALF
SPAN = WINDOW + FINE - 1
FAR_SPAN = SIDE - 1
ROWS = 208
WIDE = 256
TOP = WINDOW * SIDE
OFFSET = CELLS - (WINDOW + (FINE - WINDOW) // 2) * SIDE
NEAR = CELLS - OFFSET
SLOTS = 192
LANES = 128
GROUP = LANES // HEAD_DIM
PAIR = 2
MANY = 4
SCALE = HEAD_DIM**-0.5
TO_LOG2 = SCALE * 1.4426950408889634
LINE = 384
CENTRE = 192
FAR_CENTRE = 64
FAR_ROW = NEAR // 8 * 8

BF = jnp.bfloat16
F32 = jnp.float32


def nn(a, b, **kw):
    return lax.dot_general(a, b, (((1,), (0,)), ((), ())), preferred_element_type=F32, **kw)


def nt(a, b, **kw):
    return lax.dot_general(a, b, (((1,), (1,)), ((), ())), preferred_element_type=F32, **kw)


def split(v):
    high = v.astype(BF)
    return high, (v - high.astype(F32)).astype(BF)


def cost(micros, bytes_accessed=0):
    return pl.CostEstimate(
        flops=int(micros * 1.15e9), bytes_accessed=bytes_accessed, transcendentals=0
    )


def params(mebibytes):
    return pltpu.CompilerParams(vmem_limit_bytes=mebibytes * 2**20)


def kinds():
    q = np.arange(CELLS)
    qr, qc = q // SIDE, q % SIDE
    margin = (FINE - WINDOW) // 2
    low_r, low_c = qr // WINDOW * WINDOW - margin, qc // WINDOW * WINDOW - margin
    key = np.arange(NEAR)[:, None] + np.where(q < TOP, 0, OFFSET)[None]
    kr, kc = key // SIDE, key % SIDE
    inside = (kr >= low_r) & (kr < low_r + FINE) & (kc >= low_c) & (kc < low_c + FINE)
    kind = np.zeros((SLOTS, WIDE), np.int32)
    kind[:NEAR, :CELLS] = np.where(inside, np.where(qc >= kc, 1, 2), 0)
    kind[NEAR : NEAR + POOL] = 3
    col = np.arange(POOL) % HALF
    far = np.zeros((SLOTS - FAR_ROW, LANES), np.int32)
    shift = NEAR - FAR_ROW
    far[shift : shift + POOL, :POOL] = np.where(col[None] >= col[:, None], 1, 2)
    spread = np.zeros((LANES, WIDE), np.float32)
    spread[qr // 2 * HALF + qc // 2, q] = 1.0
    return kind, far, spread


def pooling():
    rows = SLOTS - FAR_ROW
    shift = NEAR - FAR_ROW
    token = np.arange(CELLS)
    out = np.zeros((2 * rows, ROWS), np.float32)
    for half in range(2):
        for i in range(shift):
            out[rows * half + i, FAR_ROW + i + OFFSET * half] = 1.0
        out[rows * half + shift + token // SIDE // 2 * HALF + token % SIDE // 2, token] = 0.25
    return out


def head_rows():
    lane = np.arange(2 * LANES) % LANES // HEAD_DIM
    return (lane[None] == np.arange(8)[:, None]).astype(np.float32)


def table_lines(tables):
    heads = tables.shape[0]
    fine = tables[:, : SPAN * SPAN].reshape(heads, SPAN, SPAN)[:, ::-1, ::-1]
    far = tables[:, SPAN * SPAN :].reshape(heads, FAR_SPAN, FAR_SPAN)

    def lines(part, pitch, lanes, centre):
        reach = part.shape[1] // 2
        right = jnp.pad(part[:, :, reach:], ((0, 0), (0, 0), (0, pitch - reach - 1)))
        left = jnp.pad(part[:, :, :reach], ((0, 0), (0, 0), (pitch - reach, 0)))
        start = centre - pitch * reach
        size = pitch * part.shape[1]
        right = jnp.pad(right.reshape(heads, size), ((0, 0), (start, lanes - start - size)))
        start = start - pitch
        left = jnp.pad(left.reshape(heads, size), ((0, 0), (start, lanes - start - size)))
        return right, left

    both = lines(fine, SIDE, LINE, CENTRE) + lines(far, HALF, LANES, FAR_CENTRE)
    return jnp.concatenate(both, axis=1)


def table_from_lines(right, left, far_right, far_left):
    heads = right.shape[0]

    def part(right, left, count, pitch, centre):
        reach = count // 2
        start = centre - pitch * reach
        size = pitch * count
        right = right[:, start : start + size].reshape(heads, count, pitch)[:, :, : reach + 1]
        start = start - pitch
        left = left[:, start : start + size].reshape(heads, count, pitch)[:, :, pitch - reach :]
        return jnp.concatenate([left, right], axis=2)

    fine = part(right, left, SPAN, SIDE, CENTRE)[:, ::-1, ::-1]
    far = part(far_right, far_left, FAR_SPAN, HALF, FAR_CENTRE)
    return jnp.concatenate([fine.reshape(heads, -1), far.reshape(heads, -1)], axis=1)


def spread_kernel(line_ref, kind_ref, far_kind_ref, spread_ref, out_ref):
    kind = kind_ref[...]
    far_kind = far_kind_ref[...]
    tiles = FAR_ROW // 8 + 1
    down = OFFSET // 8
    near_kind = kind[: 8 * tiles]
    lower = lax.broadcasted_iota(jnp.int32, (8, WIDE), 1) >= TOP
    shift = FAR_CENTRE + NEAR - FAR_ROW
    far_tiles = far_kind_ref.shape[0] // 8

    def stacked(part, tiles, centre, lanes):
        size = part.shape[1]
        base = pltpu.roll(jnp.broadcast_to(part, (8, size)), 0, 1, stride=1, stride_axis=0)
        return [pltpu.roll(base, (8 * t - centre) % size, 1)[:, :lanes] for t in range(tiles)]

    for h in range(GROUP):
        line = line_ref[0, h : h + 1]
        sides = []
        for start in (0, LINE):
            rolled = stacked(line[:, start : start + LINE], tiles + down, CENTRE, WIDE)
            sides.append(
                jnp.concatenate(
                    [jnp.where(lower, rolled[t + down], rolled[t]) for t in range(tiles)], axis=0
                )
            )
        fine = jnp.where(near_kind == 1, sides[0], jnp.where(near_kind == 2, sides[1], -1e9))
        far_line = line[:, 2 * LINE :]
        far_right = jnp.concatenate(stacked(far_line[:, :LANES], far_tiles, shift, LANES), axis=0)
        far_left = jnp.concatenate(stacked(far_line[:, LANES:], far_tiles, shift, LANES), axis=0)
        far = jnp.where(far_kind == 1, far_right, jnp.where(far_kind == 2, far_left, 0.0))
        far = nn(far, spread_ref[...], precision=lax.Precision.HIGHEST)
        rest = jnp.concatenate(
            [fine[FAR_ROW:], jnp.full((SLOTS - 8 * tiles, WIDE), -1e9, F32)], axis=0
        )
        out_ref[h, :FAR_ROW] = fine[:FAR_ROW] * (1.0 / SCALE)
        out_ref[h, FAR_ROW:] = jnp.where(kind[FAR_ROW:] == 3, far, rest) * (1.0 / SCALE)


def spread_tables(lines):
    heads = lines.shape[0]
    constants = [jnp.asarray(v) for v in kinds()]
    lines = lines.reshape(heads // GROUP, GROUP, -1)
    return pl.pallas_call(
        spread_kernel,
        grid=(heads // GROUP,),
        in_specs=[pl.BlockSpec((1,) + lines.shape[1:], lambda g: (g, 0, 0))]
        + [pl.BlockSpec(v.shape, lambda g: (0, 0)) for v in constants],
        out_specs=pl.BlockSpec((GROUP, SLOTS, WIDE), lambda g: (g, 0, 0)),
        out_shape=pltpu.HBM((heads, SLOTS, WIDE), F32),
        compiler_params=params(16),
        cost_estimate=cost(7),
        name="spread_tables",
    )(lines, *constants)


def unskew(tiles, lanes, centre):
    count = lanes // LANES
    wide = tiles[0].shape[1] // LANES
    zero = jnp.zeros((8, LANES), F32)
    total = [zero] * count
    lane = lax.broadcasted_iota(jnp.int32, (8, LANES), 1)
    for t, tile in enumerate(tiles):
        shift = (centre - 8 * t) % lanes
        first, part = shift // LANES, shift % LANES
        pieces = [tile[:, LANES * i : LANES * i + LANES] for i in range(wide)]
        if part:
            pieces = [pltpu.roll(v, part, 1) for v in pieces]
            pieces = [
                jnp.where(lane < part, left, right)
                for left, right in zip([zero] + pieces, pieces + [zero])
            ]
        for i, v in enumerate(pieces):
            total[(first + i) % count] = total[(first + i) % count] + v
    total = jnp.concatenate(total, axis=1)
    row = lax.broadcasted_iota(jnp.int32, (8, lanes), 0)
    out = jnp.where(row == 0, total, 0.0)
    for s in range(1, 8):
        out = out + jnp.where(row == s, pltpu.roll(total, lanes - s, 1), 0.0)
    return jnp.sum(out, axis=0, keepdims=True)


def collect(grad, side, kind_ref, far_kind_ref, spread_ref):
    tiles = FAR_ROW // 8 + 1
    down = OFFSET // 8
    part = jnp.where(kind_ref[: 8 * tiles] == side, grad[: 8 * tiles], 0.0)
    lower = lax.broadcasted_iota(jnp.int32, (8, WIDE), 1) >= TOP
    rows = [part[8 * t : 8 * t + 8] for t in range(tiles)]
    zero = jnp.zeros((8, WIDE), F32)
    both = [
        jnp.where(lower, low, high)
        for high, low in zip(rows + [zero] * down, [zero] * down + rows)
    ]
    far = grad[FAR_ROW:]
    high = far.astype(BF)
    rest = far - high.astype(F32)
    middle = rest.astype(BF)
    low = (rest - middle.astype(F32)).astype(BF)
    count = far.shape[0]
    far = nt(jnp.concatenate([high, middle, low], axis=0), spread_ref[...].astype(BF))
    far = far[:count] + far[count : 2 * count] + far[2 * count :]
    far = jnp.where(far_kind_ref[...] == side, far, 0.0)
    shift = FAR_CENTRE + NEAR - FAR_ROW
    far = [far[8 * t : 8 * t + 8] for t in range(count // 8)]
    return unskew(both, LINE, CENTRE), unskew(far, LANES, shift)


def norm_parts(stream):
    center = stream - jnp.mean(stream, axis=-1, keepdims=True)
    spread = jnp.mean(center * center, axis=-1, keepdims=True)
    rate = lax.rsqrt(spread + 1e-05)
    return center * rate, rate


def norm_back(unit, rate, gain, grad):
    inner = grad * gain
    mean = jnp.mean(inner, axis=-1, keepdims=True)
    along = jnp.mean(inner * unit, axis=-1, keepdims=True)
    return rate * (inner - mean - unit * along)


def tall(v):
    return jnp.concatenate([v, jnp.zeros((WIDE - v.shape[0], v.shape[1]), v.dtype)], axis=0)


def with_ones(v):
    return jnp.concatenate([v.T, jnp.ones((16, v.shape[0]), v.dtype)], axis=0)


def row_sum(v):
    return jnp.sum(v, axis=0, keepdims=True)


def prepare_kernel(core_ref, tokens_ref, cot_ref, x_ref, g_ref):
    images = x_ref.shape[0]
    for i in range(images):
        start = CELLS * i
        low = start // 16 * 16
        keep = lax.broadcasted_iota(jnp.int32, (ROWS, 1), 0) < CELLS
        for ref, out in ((tokens_ref, x_ref), (cot_ref, g_ref)):
            span = min(ROWS + 16, ref.shape[0] - low)
            v = ref[low : low + span].astype(F32)[start - low :]
            if v.shape[0] < ROWS:
                v = jnp.concatenate([v, jnp.zeros((ROWS - v.shape[0], v.shape[1]), F32)], axis=0)
            out[i] = jnp.where(keep, v[:ROWS], 0.0).astype(BF)


def prepare(tokens, cotangent, core):
    rows, width = cotangent.shape
    images = rows // CELLS
    padded = jax.ShapeDtypeStruct((images, ROWS, width), BF)
    whole = lambda shape: pl.BlockSpec(shape, lambda s, core: (0,) * len(shape))
    return pl.pallas_call(
        prepare_kernel,
        grid_spec=pltpu.PrefetchScalarGridSpec(
            num_scalar_prefetch=1,
            grid=(1,),
            in_specs=[
                pl.BlockSpec((rows, width), lambda s, core: (core[0], 0)),
                whole((rows, width)),
            ],
            out_specs=[whole(padded.shape)] * 2,
        ),
        out_shape=[padded] * 2,
        compiler_params=params(24),
        cost_estimate=cost(4),
        name="prepare",
    )(core, tokens, cotangent)


def shard_kernel(input_ref, output_t_ref, expand_t_ref, shrink_ref, out_ref):
    pack = jnp.concatenate([input_ref[t] for t in range(3)] + [output_t_ref[...]], axis=1)
    feed_part = jnp.concatenate([expand_t_ref[...], shrink_ref[...]], axis=1)
    out_ref[...] = jnp.concatenate([pack, feed_part], axis=0).astype(BF)


def shard(input_weight, output_t, expand_t, shrink):
    rows = output_t.shape[0] + shrink.shape[0]
    return pl.pallas_call(
        shard_kernel,
        out_shape=jax.ShapeDtypeStruct((rows, 2 * shrink.shape[1]), BF),
        compiler_params=params(60),
        cost_estimate=cost(1),
        name="shard",
    )(input_weight, output_t, expand_t, shrink)


def update_kernel(grad_ref, *refs):
    half = refs[0].shape[2]
    ins, outs = refs[:8], refs[8:]
    for t in range(3):
        grad = grad_ref[:, half * t : half * t + half]
        new = adamw(ins[0][t], grad, ins[1][t], ins[2][t], ins[3][t], 0.06, 0.05)
        for ref, value in zip(outs[:5], new + (new[0].astype(BF),)):
            ref[t] = value
    grad = grad_ref[:, 3 * half :]
    new = adamw(ins[4][...], grad, ins[5][...], ins[6][...], ins[7][...], 0.3, 0.05)
    for ref, value in zip(outs[5:], new + (new[0].astype(BF),)):
        ref[...] = value


def update(grad, inputs, outputs_t):
    shapes = []
    for v in (inputs[0], outputs_t[0]):
        shapes += [jax.ShapeDtypeStruct(v.shape, F32)] * 4 + [jax.ShapeDtypeStruct(v.shape, BF)]
    return pl.pallas_call(
        update_kernel,
        out_shape=shapes,
        compiler_params=params(16),
        cost_estimate=cost(1),
        name="update",
    )(grad, *inputs, *outputs_t)


def lanes_of(g, size=LANES):
    return pl.ds(pl.multiple_of(g * size, size), size)


def rows_of(g, h, size):
    return pl.ds(pl.multiple_of((g * GROUP + h) * size, size), size)


def place_of(core_ref, a, size):
    away = core_ref[1] ^ a
    out = 0
    for stride, radix in phases(size):
        out = out * radix + ((away >> (stride.bit_length() - 1)) & (radix - 1))
    return out


def assemble(core_ref, near_ref, far_ref, raw_s, win_s, wo_s, wint_ref, wot_ref):
    blocks, rows = near_ref.shape[0], near_ref.shape[1]
    width = wot_ref.shape[0]
    half = width // 2
    core = core_ref[0]
    for a in range(blocks):
        place = place_of(core_ref, a, blocks)
        raw_s[core, rows * a : rows * a + rows] = near_ref[place].astype(F32)
        raw_s[1 - core, rows * a : rows * a + rows] = far_ref[place].astype(F32)
    for t in range(4):
        whole = jnp.concatenate(
            [raw_s[h, :, half * t : half * t + half] for h in range(2)], axis=1
        ).astype(BF)
        if t < 3:
            win_s[:, width * t : width * t + width] = whole
            wint_ref[width * t : width * t + width] = whole.T
        else:
            wot_ref[...] = whole
            wo_s[...] = whole.T


def by_half(top, bottom):
    parts = []
    for g in range(top.shape[1] // LANES):
        lanes = slice(LANES * g, LANES * g + LANES)
        parts += [top[:, lanes], bottom[:, lanes]]
    return jnp.concatenate(parts, axis=1)


def to_slots(mixed, pool):
    high, low = split(mixed)
    far = nn(pool, jnp.concatenate([high, low], axis=0))
    rows = SLOTS - FAR_ROW
    top = jnp.concatenate([mixed[:FAR_ROW], far[:rows]], axis=0).astype(BF)
    bottom = jnp.concatenate([mixed[OFFSET : OFFSET + FAR_ROW], far[rows:]], axis=0).astype(BF)
    width = mixed.shape[1] // 2
    return [by_half(top[:, :width], bottom[:, :width]), by_half(top[:, width:], bottom[:, width:])]


def from_slots(grads, pool_t):
    groups = grads[0].shape[1] // WIDE
    top, bottom = (
        jnp.concatenate(
            [
                grad[:, WIDE * g + LANES * i : WIDE * g + LANES * i + LANES]
                for grad in grads
                for g in range(groups)
            ],
            axis=1,
        )
        for i in range(2)
    )
    high, low = split(jnp.concatenate([top[FAR_ROW:], bottom[FAR_ROW:]], axis=0))
    out = nn(pool_t, jnp.concatenate([high, low], axis=0))
    zeros = lambda count: jnp.zeros((count, top.shape[1]), F32)
    return (
        out
        + jnp.concatenate([top[:FAR_ROW], zeros(ROWS - FAR_ROW)], axis=0)
        + jnp.concatenate(
            [zeros(OFFSET), bottom[:FAR_ROW], zeros(ROWS - FAR_ROW - OFFSET)], axis=0
        )
    )


def turned(slots_ref, target_ref):
    flat = slots_ref[...].T
    for g in range(flat.shape[0] // WIDE):
        for h in range(GROUP):
            for i in range(2):
                source = WIDE * g + LANES * i + HEAD_DIM * h
                target = 2 * HEAD_DIM * (GROUP * g + h) + HEAD_DIM * i
                target_ref[target : target + HEAD_DIM] = flat[source : source + HEAD_DIM]


def masked(source, heads_ref, target_ref):
    for h in range(GROUP):
        target_ref[SLOTS * h : SLOTS * h + SLOTS] = source * heads_ref[h : h + 1]


def sides_of_lanes(v, target_ref):
    lane = lax.broadcasted_iota(jnp.int32, v.shape, 1)
    zero = jnp.zeros_like(v)
    target_ref[:LANES] = jnp.where(lane < TOP, v, zero)
    target_ref[LANES:] = jnp.where(lane < TOP, zero, v)


def choose_half(pair):
    lane = lax.broadcasted_iota(jnp.int32, (HEAD_DIM, WIDE), 1)
    return jnp.where(lane < TOP, pair[:HEAD_DIM], pair[HEAD_DIM:])


HALVES = [slice(0, LANES), slice(LANES, WIDE)]


def forward_kernel(
    core_ref,
    keep_ref,
    near_ref,
    far_ref,
    x_ref,
    vec_ref,
    bias_ref,
    pool_ref,
    heads_ref,
    state_ref,
    att_ref,
    p_ref,
    q_ref,
    k_ref,
    v_ref,
    wint_ref,
    wot_ref,
    raw_s,
    win_s,
    wo_s,
    s_s,
    km_s,
    qb_s,
    vt_s,
    att_t,
    qt_s,
):
    step = pl.program_id(0)
    width = wot_ref.shape[0]
    groups = width // LANES

    @pl.when(step == 0)
    def _():
        assemble(core_ref, near_ref, far_ref, raw_s, win_s, wo_s, wint_ref, wot_ref)

    x = x_ref[...].reshape(PAIR * ROWS, width).astype(F32)
    ln = (norm_parts(x)[0] * vec_ref[0:1] + vec_ref[1:2]).astype(BF)
    mixed = nn(ln, win_s[...])
    for b in range(PAIR):
        own = mixed[ROWS * b : ROWS * b + ROWS]
        query = (own[:, :width] + vec_ref[2:3]).astype(BF)
        q_ref[b] = query
        qt_s[b] = tall(query).T
        shift = jnp.concatenate([jnp.zeros((1, width), F32), vec_ref[3:4]], axis=1)
        k_ref[b], v_ref[b] = to_slots(own[:, width:] + shift, pool_ref[...])
        turned(v_ref.at[b], vt_s.at[b])

    def products(g):
        for b in range(PAIR):
            slot = g % 2 * PAIR + b
            masked(k_ref[b, :, WIDE * g : WIDE * g + WIDE], heads_ref, km_s.at[slot])
            sides_of_lanes(qt_s[b, LANES * g : LANES * g + LANES], qb_s.at[slot])
            s_s[slot] = nn(km_s[slot], qb_s[slot])

    products(0)
    for g in range(groups):
        if g + 1 < groups:
            products(g + 1)
        for b in range(PAIR):
            for h in range(GROUP):
                n = g * GROUP + h
                slots = slice(SLOTS * h, SLOTS * h + SLOTS)
                for half in HALVES:
                    scores = s_s[g % 2 * PAIR + b, slots, half] + bias_ref[n, :, half]
                    top = jnp.max(scores, axis=0, keepdims=True)
                    weights = jnp.exp2((scores - top) * TO_LOG2)
                    total = jnp.sum(weights, axis=0, keepdims=True)
                    p_ref[b, n, :, half] = (weights * (1.0 / total)).astype(BF)
                both = nn(vt_s[b, 2 * HEAD_DIM * n : 2 * HEAD_DIM * (n + 1)], p_ref[b, n])
                att_t[b, HEAD_DIM * n : HEAD_DIM * (n + 1)] = choose_half(both).astype(BF)

    for b in range(PAIR):
        att_ref[b] = att_t[b].T[:ROWS]
    branch = nn(att_ref[...].reshape(PAIR * ROWS, width), wo_s[...]) + vec_ref[4:5]
    for b in range(PAIR):
        scale = DROP_SCALE * keep_ref[step * PAIR + b, 0].astype(F32)
        own = branch[ROWS * b : ROWS * b + ROWS]
        state_ref[b] = x_ref[b].astype(F32) + scale * own


def attend_forward(core, flags, near, far, x, vectors, bias):
    images, _, width = x.shape
    fixed = lambda shape: pl.BlockSpec(shape, lambda s, *_: (0,) * len(shape))
    pair = lambda *shape: pl.BlockSpec((PAIR,) + shape, lambda s, *_: (s,) + (0,) * len(shape))
    pool = np.concatenate([pooling()] * 2, axis=1)
    shapes = [
        ((images, ROWS, width), F32),
        ((images, ROWS, width), BF),
        ((images,) + bias.shape, BF),
        ((images, ROWS, width), BF),
        ((images, SLOTS, 2 * width), BF),
        ((images, SLOTS, 2 * width), BF),
        ((3 * width, width), BF),
        ((width, width), BF),
    ]
    return pl.pallas_call(
        forward_kernel,
        grid_spec=pltpu.PrefetchScalarGridSpec(
            num_scalar_prefetch=2,
            grid=(images // PAIR,),
            in_specs=[
                fixed(near.shape),
                fixed(far.shape),
                pair(ROWS, width),
                fixed(vectors.shape),
                fixed(bias.shape),
                fixed(pool.shape),
                fixed((8, WIDE)),
            ],
            out_specs=[
                pair(ROWS, width),
                pair(ROWS, width),
                pair(*bias.shape),
                pair(ROWS, width),
                pair(SLOTS, 2 * width),
                pair(SLOTS, 2 * width),
                fixed((3 * width, width)),
                fixed((width, width)),
            ],
            scratch_shapes=[
                pltpu.VMEM((2, width, 2 * width), F32),
                pltpu.VMEM((width, 3 * width), BF),
                pltpu.VMEM((width, width), BF),
                pltpu.VMEM((2 * PAIR, GROUP * SLOTS, WIDE), F32),
                pltpu.VMEM((2 * PAIR, GROUP * SLOTS, WIDE), BF),
                pltpu.VMEM((2 * PAIR, WIDE, WIDE), BF),
                pltpu.VMEM((PAIR, 2 * width, SLOTS), BF),
                pltpu.VMEM((PAIR, width, WIDE), BF),
                pltpu.VMEM((PAIR, width, WIDE), BF),
            ],
        ),
        out_shape=[pltpu.HBM(s, d) for s, d in shapes],
        compiler_params=params(60),
        cost_estimate=cost(25),
        name="attend_forward",
    )(
        core,
        flags,
        near,
        far,
        x,
        vectors,
        bias,
        jnp.asarray(pool, BF),
        jnp.asarray(head_rows(), BF),
    )


def feed_kernel(
    core_ref,
    keep_ref,
    state_ref,
    g_ref,
    att_ref,
    ff0_ref,
    ff1_ref,
    wot_ref,
    vec_ref,
    fb_ref,
    result_ref,
    grad_ref,
    dout_ref,
    dff0_ref,
    dff1_ref,
    dwot_ref,
    rows_ref,
    ws_s,
    we_s,
    ff0_s,
    ff1_s,
):
    step = pl.program_id(0)
    last = pl.num_programs(0) - 1
    width = wot_ref.shape[0]
    chunks = 2 * dff0_ref.shape[0] // width
    blocks, block = ff0_ref.shape[0], ff0_ref.shape[1]
    count = MANY * ROWS

    @pl.when(step == 0)
    def _():
        ws_s[...] = jnp.zeros_like(ws_s)
        we_s[...] = jnp.zeros_like(we_s)
        dwot_ref[...] = jnp.zeros_like(dwot_ref)
        rows_ref[...] = jnp.zeros_like(rows_ref)
        for a in range(blocks):
            place = place_of(core_ref, a, blocks)
            here = slice(block * a, block * a + block)
            ff0_s[here] = ff0_ref[place]
            ff1_s[here] = ff1_ref[place]

    def column(which):
        row = lax.broadcasted_iota(jnp.int32, (count, 1), 0)
        out = keep_ref[step * MANY, which].astype(F32)
        for b in range(1, MANY):
            out = jnp.where(row < b * ROWS, out, keep_ref[step * MANY + b, which].astype(F32))
        return jnp.broadcast_to(out * DROP_SCALE, (count, 1))

    state = state_ref[...].reshape(count, width)
    upstream = g_ref[...].reshape(count, width).astype(F32)
    unit, rate = norm_parts(state)
    gain = vec_ref[5:6]
    ln = (unit * gain + vec_ref[6:7]).astype(BF)
    keep = column(1)
    scaled = keep * upstream
    signal = scaled.astype(BF)
    ln_t = with_ones(ln)
    signal_t = signal.T

    out = jnp.zeros((count, width), F32)
    grad_ln = jnp.zeros((count, width), F32)
    for c in range(chunks):
        piece = slice(width * c, width * c + width)
        ff_s = ff0_s if c < chunks // 2 else ff1_s
        here = slice(width * (c % (chunks // 2)), width * (c % (chunks // 2)) + width)
        we, ws = ff_s[here, :width], ff_s[here, width:]
        row = (c + core_ref[0] * (chunks // 2)) % chunks
        pre = nt(ln, we) + fb_ref[pl.ds(row, 1)]
        part = 0.5 * (1.0 + lax.erf(pre * np.float32(0.5**0.5)))
        act = (pre * part).astype(BF)
        slope = part + pre * (jnp.exp(-0.5 * pre * pre) * np.float32((2 * np.pi) ** -0.5))
        grad_pre = (nt(signal, ws) * slope).astype(BF)
        out = out + nn(act, ws)
        grad_ln = grad_ln + nn(grad_pre, we)
        ws_s[:, piece] += nn(signal_t, act)
        part = nn(ln_t, grad_pre)
        we_s[:, piece] += part[:width]
        rows_ref[pl.ds(4 + row, 1)] += part[width : width + 1]

    result = state + keep * (out + vec_ref[7:8])
    grad_state = upstream + norm_back(unit, rate, gain, grad_ln)
    for b in range(MANY):
        result_ref[CELLS * b : CELLS * b + CELLS] = result[ROWS * b : ROWS * b + CELLS]
    grad_ref[...] = grad_state.reshape(MANY, ROWS, width)
    scaled_one = column(0) * grad_state
    one = scaled_one.astype(BF)
    dout_ref[...] = nn(one, wot_ref[...]).astype(BF).reshape(MANY, ROWS, width)
    dwot_ref[...] += nn(one.T, att_ref[...].reshape(count, width))
    rows_ref[0:1] += row_sum(scaled_one)
    rows_ref[1:2] += row_sum(grad_ln * unit)
    rows_ref[2:3] += row_sum(grad_ln)
    rows_ref[3:4] += row_sum(scaled)

    @pl.when(step == last)
    def _():
        half = chunks // 2
        for c in range(chunks):
            piece = slice(width * c, width * c + width)
            here = slice(width * (c % half), width * (c % half) + width)
            target = dff0_ref if c < half else dff1_ref
            target[here, :width] = we_s[:, piece].astype(BF).T
            target[here, width:] = ws_s[:, piece].astype(BF).T


def feed(core, flags, state, g, att, ff0, ff1, wot, vectors, fb):
    images, _, width = state.shape
    hidden = 2 * ff0.shape[0] * ff0.shape[1]
    fixed = lambda shape: pl.BlockSpec(shape, lambda s, *_: (0,) * len(shape))
    pair = lambda *shape: pl.BlockSpec((MANY,) + shape, lambda s, *_: (s,) + (0,) * len(shape))
    shapes = [
        ((images * CELLS, width), F32),
        ((images, ROWS, width), F32),
        ((images, ROWS, width), BF),
        ((hidden // 2, 2 * width), BF),
        ((hidden // 2, 2 * width), BF),
        ((width, width), F32),
        ((8, width), F32),
    ]
    return pl.pallas_call(
        feed_kernel,
        grid_spec=pltpu.PrefetchScalarGridSpec(
            num_scalar_prefetch=2,
            grid=(images // MANY,),
            in_specs=[
                pair(ROWS, width),
                pair(ROWS, width),
                pair(ROWS, width),
                fixed(ff0.shape),
                fixed(ff1.shape),
                fixed((width, width)),
                fixed(vectors.shape),
                fixed(fb.shape),
            ],
            out_specs=[
                pl.BlockSpec((MANY * CELLS, width), lambda s, *_: (s, 0)),
                pair(ROWS, width),
                pair(ROWS, width),
                fixed((hidden // 2, 2 * width)),
                fixed((hidden // 2, 2 * width)),
                fixed((width, width)),
                fixed((8, width)),
            ],
            scratch_shapes=[
                pltpu.VMEM((width, hidden), F32),
                pltpu.VMEM((width, hidden), F32),
                pltpu.VMEM((hidden // 2, 2 * width), BF),
                pltpu.VMEM((hidden // 2, 2 * width), BF),
            ],
        ),
        out_shape=[jax.ShapeDtypeStruct(s, d) for s, d in shapes],
        compiler_params=params(56),
        cost_estimate=cost(35),
        name="feed",
    )(core, flags, state, g, att, ff0, ff1, wot, vectors, fb)


def add_kernel(one_ref, two_ref, out_ref):
    out_ref[...] = one_ref[...] + two_ref[...]


def add(one, two):
    rows, lanes = one.shape
    block = pl.BlockSpec((rows // 2, lanes), lambda s: (s, 0))
    return pl.pallas_call(
        add_kernel,
        grid=(2,),
        in_specs=[block, block],
        out_specs=block,
        out_shape=jax.ShapeDtypeStruct(one.shape, one.dtype),
        compiler_params=params(16),
        cost_estimate=cost(1.5),
        name="add",
    )(one, two)


def diagonal(whole):
    lane = lax.broadcasted_iota(jnp.int32, (SLOTS, WIDE), 1) % LANES
    out = whole[SLOTS * (GROUP - 1) :]
    for h in reversed(range(GROUP - 1)):
        out = jnp.where(lane < HEAD_DIM * (h + 1), whole[SLOTS * h : SLOTS * h + SLOTS], out)
    return out


def sides_of_rows(v, target_ref):
    row = lax.broadcasted_iota(jnp.int32, v.shape, 0)
    zero = jnp.zeros_like(v)
    target_ref[:, :LANES] = jnp.where(row < TOP, v, zero)
    target_ref[:, LANES:] = jnp.where(row < TOP, zero, v)


def small_rows(lines_ref, vector_rows, core):
    groups = lines_ref.shape[0]
    heads = groups * GROUP
    lanes = 2 * LINE
    first, rest = [], []
    for i in range(heads):
        g, h = i // GROUP, i % GROUP
        pair = [lines_ref[g, side, h : h + 1] for side in range(2)]
        first.append(jnp.concatenate([v[:, :LINE] for v in pair], axis=1))
        rest += [v[:, LINE:] for v in pair]
    per_row = lanes // LANES
    rest = [jnp.concatenate(rest[i : i + per_row], axis=1) for i in range(0, len(rest), per_row)]
    sums = [
        jnp.concatenate([vector_rows[i : i + 1], vector_rows[i + 1 : i + 2]], axis=1)
        for i in range(0, vector_rows.shape[0], 2)
    ]
    halves = [
        jnp.concatenate(
            [
                row
                for rows in (first, rest, sums)
                for row in rows[len(rows) // 2 * c : len(rows) // 2 * (c + 1)]
            ],
            axis=0,
        )
        for c in range(2)
    ]
    return jnp.where(core == 0, halves[0], halves[1])


def backward_kernel(
    core_ref,
    x_ref,
    grad_ref,
    dout_ref,
    q_ref,
    k_ref,
    v_ref,
    p_ref,
    wint_ref,
    vec_ref,
    dwot_ref,
    rows_two_ref,
    pool_t_ref,
    heads_ref,
    kind_ref,
    far_kind_ref,
    spread_ref,
    igrad_ref,
    near_ref,
    far_ref,
    dwin_s,
    rows_s,
    lines_s,
    dense0_s,
    dense1_s,
    dense2_s,
    dense3_s,
    k_t,
    raw_qt,
    raw_k,
    raw_v,
    mixed_s,
    whole_s,
    d_s,
    ds_s,
    vm_s,
    db_s,
    qr_s,
    dr_s,
):
    phase, step = pl.program_id(0), pl.program_id(1)
    width = wint_ref.shape[1]
    groups = width // LANES
    now, before = phase % 2, (phase + 1) % 2
    dense_refs = (dense0_s, dense1_s, dense2_s, dense3_s)

    def collect_before():
        g = jnp.maximum(phase - 1, 0)
        for h in range(GROUP):
            fine, far = collect(
                dense_refs[h][before], step + 1, kind_ref, far_kind_ref, spread_ref
            )
            lines_s[g, step, h : h + 1, :LINE] = fine
            lines_s[g, step, h : h + 1, LINE:] = far

    @pl.when((phase == 0) & (step == 0))
    def _():
        dwin_s[...] = jnp.zeros_like(dwin_s)
        rows_s[...] = jnp.zeros_like(rows_s)
        for ref in dense_refs:
            ref[...] = jnp.zeros_like(ref)

    @pl.when((phase > 0) & (phase < groups) & (step == 0))
    def _():
        for ref in dense_refs:
            ref[now] = jnp.zeros(ref.shape[1:], F32)

    @pl.when((phase > 0) & (phase < groups))
    def _():
        collect_before()

    @pl.when(phase < groups)
    def _():
        def products(i):
            for b in range(PAIR):
                n = i * PAIR + b
                keys, values = k_ref[n], v_ref[n]
                flat = keys.T
                for h in range(GROUP):
                    for side in range(2):
                        source = LANES * side + HEAD_DIM * h
                        target = HEAD_DIM * (2 * h + side)
                        k_t[i * PAIR + b, target : target + HEAD_DIM] = flat[source : source + HEAD_DIM]
                masked(values, heads_ref, vm_s.at[i * PAIR + b])
                dout = tall(dout_ref[n])
                sides_of_lanes(dout.T, db_s.at[i * PAIR + b])
                d_s[i * PAIR + b] = nn(vm_s[i * PAIR + b], db_s[i * PAIR + b])
                sides_of_rows(tall(q_ref[n]), qr_s.at[i * PAIR + b])
                sides_of_rows(dout, dr_s.at[i * PAIR + b])

        def attend(i):
            for h in range(GROUP):
                slots = slice(SLOTS * h, SLOTS * h + SLOTS)
                for half in HALVES:
                    dense = dense_refs[h][now, :, half]
                    for b in range(PAIR):
                        probs = p_ref[i * PAIR + b, h, :, half].astype(F32)
                        grad_probs = d_s[i * PAIR + b, slots, half]
                        along = jnp.sum(probs * grad_probs, axis=0, keepdims=True)
                        grad_scores = (probs * (grad_probs - along)).astype(BF)
                        ds_s[i * PAIR + b, slots, half] = grad_scores
                        dense = dense + grad_scores.astype(F32)
                    dense_refs[h][now, :, half] = dense
                for b in range(PAIR):
                    both = nn(k_t[i * PAIR + b, 2 * HEAD_DIM * h : 2 * HEAD_DIM * (h + 1)], ds_s[i * PAIR + b, slots])
                    raw_qt[step * MANY + i * PAIR + b, rows_of(phase, h, HEAD_DIM), :] = (
                        choose_half(both) * SCALE
                    ).astype(BF)
            wide = lanes_of(phase, WIDE)
            for b in range(PAIR):
                n = step * MANY + i * PAIR + b
                probs = p_ref[i * PAIR + b].reshape(GROUP * SLOTS, WIDE)
                raw_v[n, :, wide] = diagonal(nn(probs, dr_s[i * PAIR + b]))
                raw_k[n, :, wide] = diagonal(nn(ds_s[i * PAIR + b], qr_s[i * PAIR + b])) * SCALE

        products(0)
        for i in range(MANY // PAIR):
            if i + 1 < MANY // PAIR:
                products(i + 1)
            attend(i)

    @pl.when(phase == groups)
    def _():
        collect_before()
        gain = vec_ref[0:1]
        for i in range(MANY // PAIR):
            for b in range(PAIR):
                n = step * MANY + i * PAIR + b
                rows = slice(ROWS * b, ROWS * b + ROWS)
                mixed_s[rows, :width] = raw_qt[n].T[:ROWS]
                mixed_s[rows, width:] = from_slots([raw_k[n], raw_v[n]], pool_t_ref[...]).astype(BF)
            mixed = mixed_s[...]
            own = slice(PAIR * i, PAIR * i + PAIR)
            x = x_ref[own].reshape(PAIR * ROWS, width).astype(F32)
            unit, rate = norm_parts(x)
            ln = (unit * gain + vec_ref[1:2]).astype(BF)
            part = nn(with_ones(ln), mixed)
            dwin_s[...] += part[:width]
            sums = part[width:]
            grad_ln = nn(mixed, wint_ref[...])
            out = grad_ref[own].reshape(PAIR * ROWS, width) + norm_back(unit, rate, gain, grad_ln)
            for b in range(PAIR):
                n = PAIR * i + b
                igrad_ref[CELLS * n : CELLS * n + CELLS] = out[ROWS * b : ROWS * b + CELLS]
            rows_s[0:1] += row_sum(grad_ln * unit)
            rows_s[1:2] += row_sum(grad_ln)
            rows_s[2:3] += sums[:1, :width]
            rows_s[3:4] += sums[:1, 2 * width :]

    @pl.when((phase == groups) & (step == pl.num_programs(1) - 1))
    def _():
        rows = near_ref.shape[1]
        blocks = width // rows
        half = width // 2
        core = core_ref[0]
        for h in range(2):
            parts = [
                dwin_s[:, width * t + half * h : width * t + half * h + half] for t in range(3)
            ] + [dwot_ref[:, half * h : half * h + half]]
            whole_s[h] = jnp.concatenate(parts, axis=1)
        for a in range(blocks):
            place = place_of(core_ref, a, blocks)
            here = slice(rows * a, rows * a + rows)
            near_ref[place] = whole_s[core, here].astype(BF)
            far_ref[place] = whole_s[1 - core, here].astype(BF)
        sums = jnp.concatenate([rows_s[:4], rows_two_ref[...]], axis=0)
        extra = near_ref.shape[0] - blocks
        for ref, which in ((near_ref, core), (far_ref, 1 - core)):
            small = small_rows(lines_s, sums, which)
            pad = jnp.zeros((extra * rows - small.shape[0], small.shape[1]), F32)
            small = jnp.concatenate([small, pad], axis=0) if pad.shape[0] else small
            for i in range(extra):
                ref[blocks + i] = small[rows * i : rows * i + rows].astype(BF)


SMALL = 11


def attend_backward(
    core, pack_shape, x, grad, dout, q, k, v, probs, win_t, vectors, dwot, rows_two
):
    images, _, width = x.shape
    groups = width // LANES
    end = images // MANY - 1
    fixed = lambda shape: pl.BlockSpec(shape, lambda p, s, *_: (0,) * len(shape))
    late = lambda *shape: pl.BlockSpec(
        (MANY,) + shape,
        lambda p, s, *_: (jnp.where(p == groups, s, 0),) + (0,) * len(shape),
    )

    def early(shape, axis):
        def where(p, s, *_):
            place = [jnp.where(p == groups, end, s)] + [0] * len(shape)
            place[axis] = jnp.minimum(p, groups - 1)
            return tuple(place)

        return pl.BlockSpec((MANY,) + shape, where)

    blocks, rows, lanes = pack_shape
    pack_shape = (blocks + -(-SMALL // rows), rows, lanes)
    pool_t = np.concatenate([pooling().T] * 2, axis=1)
    tables = kinds()
    shapes = [((images * CELLS, width), F32), (pack_shape, BF), (pack_shape, BF)]
    stack = (MANY, GROUP * SLOTS, WIDE)
    square = (MANY, WIDE, WIDE)
    return pl.pallas_call(
        backward_kernel,
        grid_spec=pltpu.PrefetchScalarGridSpec(
            num_scalar_prefetch=1,
            grid=(groups + 1, images // MANY),
            in_specs=[
                late(ROWS, width),
                late(ROWS, width),
                early((ROWS, LANES), 2),
                early((ROWS, LANES), 2),
                early((SLOTS, WIDE), 2),
                early((SLOTS, WIDE), 2),
                early((GROUP, SLOTS, WIDE), 1),
                fixed(win_t.shape),
                fixed(vectors.shape),
                fixed(dwot.shape),
                fixed(rows_two.shape),
                fixed(pool_t.shape),
                fixed((8, WIDE)),
            ]
            + [fixed(v.shape) for v in tables],
            out_specs=[
                pl.BlockSpec(
                    (MANY * CELLS, width), lambda p, s, *_: (jnp.where(p == groups, s, 0), 0)
                ),
                fixed(pack_shape),
                fixed(pack_shape),
            ],
            scratch_shapes=[
                pltpu.VMEM((width, 3 * width), F32),
                pltpu.VMEM((8, width), F32),
                pltpu.VMEM((groups, 2, GROUP, LINE + LANES), F32),
                pltpu.VMEM((2, SLOTS, WIDE), F32),
                pltpu.VMEM((2, SLOTS, WIDE), F32),
                pltpu.VMEM((2, SLOTS, WIDE), F32),
                pltpu.VMEM((2, SLOTS, WIDE), F32),
                pltpu.VMEM((MANY, WIDE, SLOTS), BF),
                pltpu.VMEM((images, width, WIDE), BF),
                pltpu.VMEM((images, SLOTS, 2 * width), F32),
                pltpu.VMEM((images, SLOTS, 2 * width), F32),
                pltpu.VMEM((PAIR * ROWS, 3 * width), BF),
                pltpu.VMEM((2, width, 2 * width), F32),
                pltpu.VMEM(stack, F32),
                pltpu.VMEM(stack, BF),
                pltpu.VMEM(stack, BF),
                pltpu.VMEM(square, BF),
                pltpu.VMEM(square, BF),
                pltpu.VMEM(square, BF),
            ],
        ),
        out_shape=[jax.ShapeDtypeStruct(s, d) for s, d in shapes],
        compiler_params=params(56),
        cost_estimate=cost(45),
        name="attend_backward",
    )(
        core,
        x,
        grad,
        dout,
        q,
        k,
        v,
        probs,
        win_t,
        vectors,
        dwot,
        rows_two,
        jnp.asarray(pool_t, BF),
        jnp.asarray(head_rows(), BF),
        *[jnp.asarray(v) for v in tables],
    )


def phases(size):
    out, stride = [], 1
    while stride < size:
        radix = 4 if size // stride % 4 == 0 else 2
        out.append((stride, radix))
        stride *= radix
    return out


def hop(v, stride, mask):
    return lax.ppermute(
        v, "dp", [(i, i ^ (mask * stride)) for i in range(lax.axis_size("dp"))]
    )


def meet(v, stride, radix):
    return jnp.stack([v] + [hop(v, stride, m) for m in range(1, radix)])


def swap(v):
    return lax.ppermute(v, "head", [(0, 1), (1, 0)])


def exchange(v):
    return lax.all_to_all(v, "dp", 0, 0)


def repeat(v, times):
    return jnp.broadcast_to(v[None], (times,) + v.shape)


def tree_sum(parts):
    while len(parts) > 1:
        parts = [parts[i] + parts[i + 1] for i in range(0, len(parts), 2)]
    return parts[0]


def reduce_parts(v, small):
    blocks, rows, lanes = v.shape
    v = v.reshape(blocks * rows, lanes)
    for stride, radix in phases(blocks):
        count = v.shape[0] // radix
        small = small.astype(BF)
        got = [
            hop(
                jnp.concatenate([v[count * m : count * m + count].astype(BF), small], axis=0),
                stride,
                m,
            ).astype(F32)
            for m in range(1, radix)
        ]
        v = tree_sum([v[:count]] + [g[:count] for g in got])
        small = tree_sum([small.astype(F32)] + [g[count:] for g in got])
    return v, small


def by_core(core, near, far):
    return jnp.where(core == 0, near, far), jnp.where(core == 0, far, near)


def adamw(weight, grad, first, second, average, rate, decay):
    first = 0.9 * first + 0.1 * grad
    second = 0.999 * second + 0.001 * grad * grad
    fix_one = 1.0 - 0.9**STEP
    fix_two = 1.0 - 0.999**STEP
    weight = weight - rate * (
        first / fix_one / (jnp.sqrt(second / fix_two) + 1e-08) + decay * weight
    )
    average = 0.9 * average + 0.1 * weight
    return (weight, first, second, average)


def shards(
    tokens,
    keep,
    cotangent,
    input_weight,
    output_weight,
    expand_weight,
    shrink_weight,
    bias_tables,
    vectors,
    first_input,
    second_input,
    average_input,
    first_output,
    second_output,
    average_output,
    first_expand,
    second_expand,
    average_expand,
    first_shrink,
    second_shrink,
    average_shrink,
    first_tables,
    second_tables,
    average_tables,
    first_vectors,
    second_vectors,
    average_vectors,
):
    dp, head = lax.axis_size("dp"), lax.axis_size("head")
    core = lax.axis_index("head")
    width = vectors.shape[1]
    own_images = cotangent.shape[0] // CELLS
    rows = input_weight.shape[1]
    hidden = expand_weight.shape[1] * dp * head
    block = hidden // (dp * head)

    part = shard(input_weight, output_weight.T, expand_weight.T, shrink_weight)
    pick = jnp.stack([core, lax.axis_index("dp")]).astype(jnp.int32)
    tables = by_core(core, bias_tables, swap(bias_tables))
    lines = table_lines(jnp.concatenate(tables, axis=0))
    x, g = prepare(tokens, cotangent, pick)
    *high, low = reversed(phases(dp))
    for stride, radix in high:
        part = meet(part, stride, radix)
    lines, part, x, g = lax.optimization_barrier((lines, part, x, g))
    bias = spread_tables(lines)
    part = part.reshape(-1, *part.shape[-2:])
    pack0 = meet(part[:, :rows], *low)
    ff, pack0, bias = lax.optimization_barrier((part[:, rows:], pack0, bias))
    pack0 = pack0.reshape(dp, rows, 2 * width)
    pack1 = swap(pack0)
    ff_parts = [ff] + [hop(ff, low[0], m) for m in range(1, low[1])]
    flags = lax.dynamic_slice_in_dim(keep, core * own_images, own_images, 0)
    fb = vectors[8:].reshape(dp, head, block).swapaxes(0, 1).reshape(-1, width)

    state, att, probs, q, k, v, win_t, wot = attend_forward(
        pick, flags, pack0, pack1, x, vectors, bias
    )
    ff_parts, state = lax.optimization_barrier((ff_parts, state))
    ff0 = jnp.concatenate(ff_parts, axis=0)
    ff1 = swap(ff0)
    result, grad_state, dout, dff0, dff1, dwot, rows_two = feed(
        pick, flags, state, g, att, ff0, ff1, wot, vectors, fb
    )
    dff = add(dff0, swap(dff1)).reshape(dp, block, 2 * width)
    dff, dout = lax.optimization_barrier((dff, dout))
    dff = exchange(dff)
    input_grad, dpack0, dpack1 = attend_backward(
        pick,
        pack0.shape,
        x,
        grad_state,
        dout,
        q,
        k,
        v,
        probs,
        win_t,
        vectors,
        dwot,
        rows_two,
    )
    dff, dpack1 = lax.optimization_barrier((dff, dpack1))
    ff_grad = jnp.sum(dff.astype(F32), axis=0)

    dpack = dpack0.astype(F32) + swap(dpack1).astype(F32)
    small = dpack[dp:].reshape(-1, 2 * width)[: -(-SMALL // 8) * 8]
    pack_grad, small = reduce_parts(dpack[:dp], small)
    local_heads = bias_tables.shape[0]
    lines = small[:local_heads]
    far = small[local_heads : local_heads + local_heads // 3].reshape(local_heads, 2, LANES)
    table_grad = table_from_lines(lines[:, :LINE], lines[:, LINE:], far[:, 0], far[:, 1])
    own_vector = small[local_heads + local_heads // 3 : SMALL]
    vector_total = jnp.concatenate(by_core(core, own_vector, swap(own_vector)))
    vector_total = vector_total.reshape(vectors.shape)
    fb_total = vector_total[8:].reshape(head, dp, block).swapaxes(0, 1).reshape(-1, width)
    vector_total = jnp.concatenate([vector_total[:8], fb_total])

    new = update(
        pack_grad,
        (input_weight, first_input, second_input, average_input),
        (output_weight.T, first_output.T, second_output.T, average_output.T),
    )
    input_new, output_new = new[:5], [v.T for v in new[5:]]
    grad_expand = ff_grad[:, :width].T
    grad_shrink = ff_grad[:, width:]
    expand_new = adamw(
        expand_weight, grad_expand, first_expand, second_expand, average_expand, 0.06, 0.05
    )
    shrink_new = adamw(
        shrink_weight, grad_shrink, first_shrink, second_shrink, average_shrink, 0.06, 0.05
    )
    tables_new = adamw(
        bias_tables, table_grad, first_tables, second_tables, average_tables, 1.0, 0.0
    )
    vectors_new = adamw(
        vectors, vector_total, first_vectors, second_vectors, average_vectors, 0.6, 0.0
    )
    return (
        result,
        input_grad,
        *input_new,
        *output_new,
        *expand_new,
        expand_new[0].astype(BF),
        *shrink_new,
        shrink_new[0].astype(BF),
        *tables_new,
        *vectors_new,
    )


def solution(mesh):
    both = P(("dp", "head"), None)
    inputs = P(None, "dp", "head")
    output = P("head", "dp")
    expand = P(None, ("dp", "head"))
    tables = P("head", None)
    in_specs = (
        (P("dp", None), P("dp", None), both, inputs, output, expand, both, tables, P())
        + (inputs,) * 3
        + (output,) * 3
        + (expand,) * 3
        + (both,) * 3
        + (tables,) * 3
        + (P(),) * 3
    )
    out_specs = (
        (both, both)
        + (inputs,) * 5
        + (output,) * 5
        + (expand,) * 5
        + (both,) * 5
        + (tables,) * 4
        + (P(),) * 4
    )
    return jax.shard_map(shards, mesh=mesh, in_specs=in_specs, out_specs=out_specs, check_vma=False)
```
